256 devices in a mesh: ctx: 32 (over x, z), head: 8 (over y, core).
Axes of the slice: x: 4, y: 4, z: 8, core: 2. Of those that a mesh axis runs over, the one named last changes fastest.
Arguments:
- x_in: bfloat16 [32768, 16384], P('ctx', 'head'), may hold values from -6 to 6
- bc_in: bfloat16 [32768, 2, 1024], P(('ctx', 'head')), may hold values from -6 to 6
- z_in: bfloat16 [32768, 16384], P('ctx', 'head'), may hold values from -6 to 6
- dt: float32 [32768, 256], P('ctx', 'head'), may hold values from 0.001 to 0.1
- log_decay: float32 [32768, 256], P('ctx', 'head'), may hold values from -1 to 0
- x_kernel: float32 [4, 16384], P(None, 'head'), may hold values from -3 to 3
- bc_kernel: float32 [4, 2, 1024], P(None, None, 'head'), may hold values from -3 to 3
- x_bias: float32 [16384], P('head'), may hold values from -1 to 0
- bc_bias: float32 [2, 1024], P(None, 'head'), may hold values from -1 to 0
- skip: float32 [256], P('head'), may hold values from 0.5 to 1.5
- norm_gain: float32 [16384], P('head'), may hold values from 0.5 to 1.5
Outputs:
- mixed: bfloat16 [32768, 16384], P('ctx', 'head')
The draws below stay inside these ranges and needn't reach their ends.
All inputs are finite; a program needn't handle non-finite values.
Results may differ from the reference program's by a relative error of at most 0.012.
Values may be sent and summed in bfloat16 or wider, within the bound.
A program may use at most 128 MiB of HBM per device.

```python
import math
import jax
import jax.numpy as jnp
from jax import lax

HEAD_COUNT = 256
HEAD_DIM = 64
STATE = 128
GROUP_COUNT = 8
KERNEL = 4
BLOCK_LENGTH = 512
WINDOW_TOKENS = 32768
INNER = 16384
GSTATE = 1024


def draw_log_decay(key, part):
    parallel_sequences = jax.random.split(jax.random.fold_in(key, 17), 8)
    fast_groups = GROUP_COUNT // 2
    heads_per_group = HEAD_COUNT // GROUP_COUNT
    number_of_blocks = WINDOW_TOKENS // BLOCK_LENGTH
    index_of_head = jnp.arange(HEAD_COUNT)
    head_to_group = index_of_head // heads_per_group
    group_order = jax.random.permutation(parallel_sequences[0], GROUP_COUNT)
    quick_group = (group_order < fast_groups)[head_to_group]
    displacements = jax.random.randint(parallel_sequences[1], (GROUP_COUNT,), 0, heads_per_group)
    dispersion = max(1, heads_per_group // 4)
    spike_head = quick_group & ((index_of_head - displacements[head_to_group]) % heads_per_group < dispersion)
    quick_head = quick_group & jnp.logical_not(spike_head)
    slow_rate = jnp.exp(jax.random.uniform(parallel_sequences[2], (HEAD_COUNT,), jnp.float32, math.log(0.05), math.log(0.7))) / WINDOW_TOKENS
    fast_rate = jax.random.uniform(parallel_sequences[3], (HEAD_COUNT,), jnp.float32, 0.0138, 0.02)
    baseline_rate = jnp.where(quick_head, fast_rate, slow_rate)
    jaggedness = jnp.exp(jax.random.uniform(parallel_sequences[4], (WINDOW_TOKENS, HEAD_COUNT), jnp.float32, math.log(0.5), math.log(2.0)))
    token_positions = jnp.arange(WINDOW_TOKENS)[:, None]
    trailing_blocks = max(1, number_of_blocks // 4)
    spike_block = jax.random.randint(parallel_sequences[7], (GROUP_COUNT,), number_of_blocks - 1 - trailing_blocks, number_of_blocks - 1)
    trailing_begin = (spike_block[head_to_group] + 1) * BLOCK_LENGTH - 14
    inside_trailing = (token_positions >= trailing_begin[None, :]) & (token_positions < (trailing_begin + 14)[None, :]) & spike_head[None, :]
    heavy_attenuation = jnp.where(inside_trailing, 6.95 / 14.0, 0.0)
    spike_locations = jax.random.randint(parallel_sequences[5], (2, HEAD_COUNT), 0, WINDOW_TOKENS)
    spike_magnitudes = jax.random.uniform(parallel_sequences[6], (2, HEAD_COUNT), jnp.float32, 0.22, 0.45)
    minor_spikes = jnp.where(token_positions == spike_locations[0][None, :], spike_magnitudes[0][None, :], 0.0)
    minor_spikes = minor_spikes + jnp.where(token_positions == spike_locations[1][None, :], spike_magnitudes[1][None, :], 0.0)
    minor_spikes = jnp.where(quick_head[None, :] | inside_trailing, 0.0, minor_spikes)
    return (-(baseline_rate[None, :] * jaggedness) - minor_spikes - heavy_attenuation).astype(jnp.float32)


def block_levels(own_key, dims, cuts, least, top_value):
    loudness = 1.0
    for position, blocks in cuts:
        steps = jax.random.uniform(jax.random.fold_in(jax.random.fold_in(own_key, 6), position), (blocks,), jnp.float32, least / len(cuts), top_value / len(cuts))
        loudness = loudness * jnp.repeat(jnp.exp(steps), dims[position] // blocks).reshape((-1,) + (1,) * (len(dims) - 1 - position))
    return loudness


def normal_values(stream_key, extent, deviation, reach, cuts=(), kind=jnp.bfloat16):
    entries = jax.random.normal(stream_key, extent, jnp.float32) * deviation
    if len(cuts) > 0:
        entries = block_levels(stream_key, extent, cuts, -0.22, 0.18) * entries
    return jnp.clip(entries, min=-reach, max=reach).astype(kind)


def setup_inputs(seed: int = 0) -> dict:
    keys = jax.random.split(jax.random.key(seed), 12)
    x_in = normal_values(keys[0], (WINDOW_TOKENS, INNER), 1.0, 6.0, ((0, 32), (1, 8)))
    bc_in = normal_values(keys[1], (WINDOW_TOKENS, 2, GSTATE), 1.0, 6.0, ((0, 256),))
    z_in = normal_values(keys[2], (WINDOW_TOKENS, INNER), 1.0, 6.0, ((0, 32), (1, 8)))
    dt = jnp.clip(jnp.exp(math.log(0.1) - 4.6051702 * jax.random.uniform(keys[3], (WINDOW_TOKENS, HEAD_COUNT), jnp.float32) ** block_levels(keys[3], (WINDOW_TOKENS, HEAD_COUNT), ((0, 32), (1, 8)), -0.2, 0.2)), 0.001, 0.1)
    log_decay = draw_log_decay(jax.random.fold_in(keys[11], 71), 0)
    x_kernel = normal_values(keys[5], (KERNEL, INNER), KERNEL ** -0.5, 3.0, ((1, 8),), jnp.float32)
    bc_kernel = normal_values(keys[6], (KERNEL, 2, GSTATE), KERNEL ** -0.5, 3.0, ((2, 8),), jnp.float32)
    x_bias = jnp.clip(-1.0 + 1.0 * jax.random.uniform(keys[7], (INNER,), jnp.float32) ** block_levels(keys[7], (INNER,), ((0, 8),), -0.2, 0.2), -1.0, 0.0)
    bc_bias = jnp.clip(-1.0 + 1.0 * jax.random.uniform(keys[8], (2, GSTATE), jnp.float32) ** block_levels(keys[8], (2, GSTATE), ((1, 8),), -0.2, 0.2), -1.0, 0.0)
    skip = jnp.clip(0.5 + 1.0 * jax.random.uniform(keys[9], (HEAD_COUNT,), jnp.float32) ** block_levels(keys[9], (HEAD_COUNT,), ((0, 8),), -0.2, 0.2), 0.5, 1.5)
    norm_gain = jnp.clip(1.0 + 0.1 * jax.random.normal(keys[10], (INNER,), jnp.float32), 0.5, 1.5)
    return dict(x_in=x_in, bc_in=bc_in, z_in=z_in, dt=dt, log_decay=log_decay, x_kernel=x_kernel, bc_kernel=bc_kernel, x_bias=x_bias, bc_bias=bc_bias, skip=skip, norm_gain=norm_gain)


def conv_silu(seq, kernel, bias):
    edge = KERNEL - 1
    padding_config = [(edge, 0)] + [(0, 0)] * (seq.ndim - 1)
    padded = jnp.pad(seq.astype(jnp.float32), padding_config)
    length = seq.shape[0]
    total = jnp.broadcast_to(bias.astype(jnp.float32), seq.shape)
    for tap in range(KERNEL):
        total = total + kernel[tap] * padded[tap:tap + length]
    return jax.nn.silu(total).astype(jnp.bfloat16)

def widen(value):
    return lax.optimization_barrier(value.astype(jnp.bfloat16)).astype(jnp.float32)

def reference(x_in, bc_in, z_in, dt, log_decay, x_kernel, bc_kernel, x_bias, bc_bias, skip, norm_gain):
    xc = conv_silu(x_in, x_kernel, x_bias)
    bcc = conv_silu(bc_in, bc_kernel, bc_bias)
    count = WINDOW_TOKENS // BLOCK_LENGTH
    heads_per_group = HEAD_COUNT // GROUP_COUNT
    x_blocks = xc.reshape(count, BLOCK_LENGTH, HEAD_COUNT, HEAD_DIM)
    b_blocks = bcc[:, 0].reshape(count, BLOCK_LENGTH, GROUP_COUNT, STATE)
    c_blocks = bcc[:, 1].reshape(count, BLOCK_LENGTH, GROUP_COUNT, STATE)
    dt_blocks = dt.reshape(count, BLOCK_LENGTH, HEAD_COUNT)
    decay_blocks = log_decay.reshape(count, BLOCK_LENGTH, HEAD_COUNT)
    places = jnp.arange(BLOCK_LENGTH)
    causal = (places[:, None] >= places[None, :])[None]

    def advance(state, pieces):
        xb, bb, cb, db, lb = pieces
        cum = jnp.cumsum(lb, axis=0)
        scores = jnp.einsum('tgn,sgn->gts', cb.astype(jnp.float32), bb.astype(jnp.float32))
        scores = jnp.repeat(scores, heads_per_group, axis=0)
        cum_h = cum.T
        gap = jnp.where(causal, cum_h[:, :, None] - cum_h[:, None, :], 0.0)
        mix = jnp.where(causal, scores * jnp.exp(gap) * db.T[:, None, :], 0.0)
        y_intra = jnp.einsum('hts,shp->thp', widen(mix), xb.astype(jnp.float32))
        c_heads = jnp.repeat(cb, heads_per_group, axis=1).astype(jnp.float32)
        c_dec = widen(c_heads * jnp.exp(cum)[:, :, None])
        y_inter = jnp.einsum('thn,hpn->thp', c_dec, widen(state))
        last = cum[-1]
        weight = jnp.exp(last[None, :] - cum) * db
        b_heads = jnp.repeat(bb, heads_per_group, axis=1).astype(jnp.float32)
        b_w = widen(b_heads * weight[:, :, None])
        fresh = jnp.einsum('thn,thp->hpn', b_w, xb.astype(jnp.float32))
        new_state = state * jnp.exp(last)[:, None, None] + fresh
        y = y_intra + y_inter + skip[None, :, None] * xb.astype(jnp.float32)
        return (new_state, y)
    start = jnp.zeros((HEAD_COUNT, HEAD_DIM, STATE), jnp.float32)
    _, outputs = lax.scan(advance, start, (x_blocks, b_blocks, c_blocks, dt_blocks, decay_blocks))
    y = outputs.reshape(WINDOW_TOKENS, HEAD_COUNT * HEAD_DIM)
    gated = y * jax.nn.silu(z_in.astype(jnp.float32))
    grouped = gated.reshape(WINDOW_TOKENS, GROUP_COUNT, -1)
    scale = lax.rsqrt(lax.optimization_barrier(jnp.mean(grouped * grouped, axis=-1, keepdims=True)) + 1e-05)
    normed = (grouped * scale).reshape(WINDOW_TOKENS, HEAD_COUNT * HEAD_DIM) * norm_gain
    return normed.astype(jnp.bfloat16)
```

```python
import functools

import jax
import jax.numpy as jnp
from jax import lax
from jax.experimental import pallas as pl
from jax.experimental.pallas import tpu as pltpu
from jax.sharding import PartitionSpec as P

MESH = pl.DeviceIdType.MESH
F32, BF16 = jnp.float32, jnp.bfloat16
HEAD_DIM = 64
STATE = 128
CHUNK = 128
HALO = 16
WIDE = 256
HIGHEST = lax.Precision.HIGHEST


def split(value):
    high = value.astype(BF16)
    low = (value - high.astype(F32)).astype(BF16)
    return jnp.concatenate([high, low], axis=0)


def across(left, right):
    return lax.dot_general(left, right, (((0,), (0,)), ((), ())), preferred_element_type=F32)


def dot(left, right):
    return jnp.dot(left, right, preferred_element_type=F32)


def swish_of_twice(half):
    return half + half * jnp.tanh(half)


def kernel(
    sizes,
    x_hbm, bc_hbm, z_hbm, dt_ref, decay_ref, xk_ref, bck_ref, xb_ref, bcb_ref, skip_ref, gain_ref,
    out_hbm,
    x_buf, xc_buf, xs_buf, z_buf, a_buf, b_buf, g_buf, out_buf,
    spread, rows, w_t, g_t, full_t, bc_buf, bc_f32, b_t, sc_buf,
    f_buf, r_buf, o_buf, ent, d_send, d_buf, e_decay,
    x_sem, z_sem, out_sem, bc_sem, hx_sem, hb_sem, d_sem, f_sem, e_sem,
):
    n_ctx, n_head, tokens, channels = sizes
    chunks, tiles = tokens // CHUNK, channels // WIDE
    heads = channels // HEAD_DIM
    share = tokens // n_head
    c, h = lax.axis_index("ctx"), lax.axis_index("head")
    following, preceding = lax.rem(c + 1, n_ctx), lax.rem(c + n_ctx - 1, n_ctx)
    last_head = n_head - 1

    barrier = pltpu.get_barrier_semaphore()

    @pl.loop(1, n_head)
    def _(d):
        pl.semaphore_signal(barrier, inc=1, device_id=(c, lax.rem(h + d, n_head)), device_id_type=MESH)

    @pl.when(h != last_head)
    def _():
        pl.semaphore_signal(barrier, inc=1, device_id=(preceding, last_head), device_id_type=MESH)

    @pl.loop(1, n_ctx)
    def _(d):
        pl.semaphore_signal(barrier, inc=1, device_id=(lax.rem(c + d, n_ctx), h), device_id_type=MESH)

    def x_copy(q):
        part = pl.ds(q * CHUNK, CHUNK)
        return pltpu.make_async_copy(
            x_hbm.at[part], x_buf.at[pl.ds(HALO + q * CHUNK, CHUNK)], x_sem.at[q]
        )

    for q in range(chunks):
        x_copy(q).start()
    z_copy = pltpu.make_async_copy(z_hbm, z_buf, z_sem)
    z_copy.start()

    d_send[...] = jnp.zeros_like(d_send)
    sums = lax.dot_general(
        jnp.ones((8, tokens), F32), decay_ref[...], (((1,), (1,)), ((), ())),
        precision=HIGHEST, preferred_element_type=F32,
    )
    d_send[:, 0:heads] = sums[0:1]
    d_buf[c] = d_send[...]

    pl.semaphore_wait(barrier, n_ctx - 1 + n_head - 1 + jnp.where(h == last_head, n_head - 1, 0))

    def columns(t):
        return pl.ds(pl.multiple_of(t * STATE, STATE), STATE)

    mine = bc_buf.at[pl.ds(HALO + h * share, share)]

    @pl.loop(1, n_head)
    def _(d):
        t = lax.rem(h + d, n_head)
        pltpu.make_async_remote_copy(
            src_ref=bc_hbm.at[:, :, columns(t)], dst_ref=mine, send_sem=bc_sem.at[0], recv_sem=bc_sem.at[1],
            device_id=(c, t), device_id_type=MESH,
        ).start()

    own_bc = pltpu.make_async_copy(bc_hbm.at[:, :, columns(h)], mine, bc_sem.at[2])
    own_bc.start()

    @pl.when(h == last_head)
    def _():
        @pl.loop(0, n_head)
        def _(t):
            pltpu.make_async_remote_copy(
                src_ref=bc_hbm.at[pl.ds(share - HALO, HALO), :, columns(t)], dst_ref=bc_buf.at[pl.ds(0, HALO)],
                send_sem=hb_sem.at[0], recv_sem=hb_sem.at[1], device_id=(following, t), device_id_type=MESH,
            ).start()

    halo_x = pltpu.make_async_remote_copy(
        src_ref=x_hbm.at[pl.ds(tokens - HALO, HALO)], dst_ref=x_buf.at[pl.ds(0, HALO)],
        send_sem=hx_sem.at[0], recv_sem=hx_sem.at[1], device_id=(following, h), device_id_type=MESH,
    )
    halo_x.start()

    @pl.loop(1, n_ctx)
    def _(d):
        pltpu.make_async_remote_copy(
            src_ref=d_send, dst_ref=d_buf.at[c], send_sem=d_sem.at[0], recv_sem=d_sem.at[1],
            device_id=(lax.rem(c + d, n_ctx), h), device_id_type=MESH,
        ).start()

    head_of = lax.broadcasted_iota(jnp.int32, (2 * heads, channels), 1) // HEAD_DIM
    row_of = lax.rem(lax.broadcasted_iota(jnp.int32, (2 * heads, channels), 0), heads)
    spread[...] = (head_of == row_of).astype(F32).astype(BF16)

    upto = (
        lax.broadcasted_iota(jnp.int32, (CHUNK, CHUNK), 0) <= lax.broadcasted_iota(jnp.int32, (CHUNK, CHUNK), 1)
    ).astype(F32)
    before = jnp.zeros((heads, 1), F32)
    to_middle, to_end = [], []
    for q in range(chunks):
        part = slice(q * CHUNK, (q + 1) * CHUNK)
        cum = jnp.dot(decay_ref[:, part], upto, precision=HIGHEST, preferred_element_type=F32)
        middle, last = cum[:, CHUNK // 2 - 1 : CHUNK // 2], cum[:, CHUNK - 1 : CHUNK]
        w_t[q] = split(jnp.exp(middle - cum) * dt_ref[:, part])
        g_t[q] = split(jnp.exp(cum - middle))
        full_t[q] = split(jnp.exp(before + cum))
        to_middle.append(jnp.exp(middle))
        to_end.append(jnp.exp(last - middle))
        before = before + last
    lane = lax.broadcasted_iota(jnp.int32, (heads, 128), 1)
    packed = jnp.zeros((heads, 128), F32)
    for i, value in enumerate(to_middle + to_end):
        packed = jnp.where(lane == i, value, packed)
    eye = lax.broadcasted_iota(jnp.int32, (heads, heads), 0) == lax.broadcasted_iota(jnp.int32, (heads, heads), 1)
    skip_column = jnp.sum(jnp.where(eye, skip_ref[...], 0.0), axis=1, keepdims=True)
    packed = split(jnp.where(lane == 2 * chunks, skip_column, packed))
    for j in range(tiles):
        wide = slice(j * WIDE, (j + 1) * WIDE)
        rows[:, wide] = across(packed, spread[:, wide])[0 : rows.shape[0]]

    halo_x.wait_recv()

    @pl.when(c == 0)
    def _():
        x_buf[0:HALO] = jnp.zeros((HALO, channels), BF16)

    for q in range(chunks):
        x_copy(q).wait()

        @pl.loop(0, tiles)
        def _(j):
            wide = pl.ds(pl.multiple_of(j * WIDE, WIDE), WIDE)
            part = slice(q * CHUNK, (q + 1) * CHUNK)
            seen = x_buf[q * CHUNK : q * CHUNK + CHUNK + HALO, wide].astype(F32)
            half = 0.5 * xb_ref[:, wide]
            for tap in range(4):
                first = HALO - 3 + tap
                half = half + (0.5 * xk_ref[tap : tap + 1, wide]) * seen[first : first + CHUNK]
            xc = swish_of_twice(half).astype(BF16)
            xc_buf[part, wide] = xc
            xs_buf[q, 0:CHUNK, wide] = (xc.astype(F32) * across(w_t[q], spread[:, wide])).astype(BF16)

    others = bc_buf.at[pl.ds(0, tokens - share)]
    pltpu.make_async_copy(others, others, bc_sem.at[1]).wait()
    own_bc.wait()
    pltpu.make_async_copy(bc_buf.at[pl.ds(0, HALO)], bc_buf.at[pl.ds(0, HALO)], hb_sem.at[1]).wait()
    flat = bc_buf.reshape(2 * (tokens + HALO), STATE)
    bc_f32[0 : 2 * HALO] = jnp.where(c == 0, 0.0, flat[0 : 2 * HALO].astype(F32))
    causal = lax.broadcasted_iota(jnp.int32, (CHUNK, CHUNK), 0) >= lax.broadcasted_iota(jnp.int32, (CHUNK, CHUNK), 1)
    for q in range(chunks):
        first = 2 * (HALO + q * CHUNK)
        bc_f32[first : first + 2 * CHUNK] = flat[first : first + 2 * CHUNK].astype(F32)
        done = []
        for which in range(2):
            half = 0.5 * bcb_ref[which : which + 1]
            for tap in range(4):
                start = 2 * (HALO + q * CHUNK - 3 + tap) + which
                half = half + (0.5 * bck_ref[tap, which : which + 1]) * bc_f32[pl.ds(start, CHUNK, stride=2), :]
            done.append(swish_of_twice(half))
        b_t[q] = done[0].T.astype(BF16)
        b_part, c_part = done[0].astype(BF16), done[1].astype(BF16)
        scores = lax.dot_general(c_part, b_part, (((1,), (1,)), ((), ())), preferred_element_type=F32)
        sc_buf[q, :, 0:CHUNK] = jnp.where(causal, scores, 0.0).astype(BF16)
        sc_buf[q, :, CHUNK : CHUNK + STATE] = c_part

    def to_owner(k):
        return pltpu.make_async_remote_copy(
            src_ref=f_buf.at[k], dst_ref=r_buf.at[c], send_sem=f_sem.at[0], recv_sem=f_sem.at[1],
            device_id=(k, h), device_id_type=MESH,
        )

    per_tile = n_ctx // tiles
    deep = STATE * 128 // (STATE * channels // n_ctx)
    height = STATE // deep

    @pl.loop(0, tiles)
    def _(i):
        j = lax.rem(i + c // per_tile, tiles)
        wide = pl.ds(pl.multiple_of(j * WIDE, WIDE), WIDE)
        state = jnp.zeros((STATE, WIDE), F32)
        for q in range(chunks):
            scaled = state * rows[q : q + 1, wide]
            xs_buf[q, CHUNK : CHUNK + STATE, wide] = scaled.astype(BF16)
            fresh = dot(b_t[q], xs_buf[q, 0:CHUNK, wide])
            state = (scaled + fresh) * rows[chunks + q : chunks + q + 1, wide]
        for a in range(WIDE // 128):
            for b in range(deep):
                f_buf[j * per_tile + a * deep + b] = state[
                    b * height : (b + 1) * height, a * 128 : (a + 1) * 128
                ].astype(BF16)
        for s in range(per_tile):
            k = j * per_tile + s

            @pl.when(k != c)
            def _():
                to_owner(k).start()

    r_buf[c] = f_buf[c]
    z_copy.wait()

    def gate(first, end):
        @pl.loop(first * tiles, end * tiles)
        def _(i):
            q, j = i // tiles, lax.rem(i, tiles)
            wide = pl.ds(pl.multiple_of(j * WIDE, WIDE), WIDE)
            part = pl.ds(pl.multiple_of(q * CHUNK, CHUNK), CHUNK)
            y = dot(sc_buf[q], xs_buf[q, :, wide]) * across(g_t[q], spread[:, wide])
            y = y + rows[2 * chunks : 2 * chunks + 1, wide] * xc_buf[part, wide].astype(F32)
            swish = swish_of_twice(0.5 * z_buf[part, wide].astype(F32))
            a_buf[part, wide] = y * swish
            b_buf[part, wide] = across(full_t[q], spread[:, wide]) * swish

    gate(0, chunks)

    pltpu.make_async_copy(d_buf.at[pl.ds(0, n_ctx - 1)], d_buf.at[pl.ds(0, n_ctx - 1)], d_sem.at[1]).wait()
    pair = c // deep
    pick = (
        lax.broadcasted_iota(jnp.int32, (128, 128), 0)
        == 2 * pair + lax.broadcasted_iota(jnp.int32, (128, 128), 1) // HEAD_DIM
    ).astype(F32)
    totals = d_buf[...].reshape(n_ctx, 128)
    e_decay[...] = jnp.exp(jnp.dot(totals, pick, precision=HIGHEST, preferred_element_type=F32))
    pltpu.make_async_copy(r_buf.at[pl.ds(0, n_ctx - 1)], r_buf.at[pl.ds(0, n_ctx - 1)], f_sem.at[1]).wait()

    def advance(i, state):
        o_buf[i] = state.astype(BF16)
        return state * e_decay[pl.ds(i, 1), :] + r_buf[i].astype(F32)

    lax.fori_loop(0, n_ctx, advance, jnp.zeros((height, 128), F32))

    place = (
        pl.ds(pl.multiple_of(lax.rem(c, deep) * height, height), height),
        pl.ds(pl.multiple_of(pair * 128, 128), 128),
    )

    @pl.loop(1, n_ctx)
    def _(d):
        t = lax.rem(c + d, n_ctx)
        pltpu.make_async_remote_copy(
            src_ref=o_buf.at[t], dst_ref=ent.at[place], send_sem=e_sem.at[0], recv_sem=e_sem.at[1],
            device_id=(t, h), device_id_type=MESH,
        ).start()

    ent[place] = o_buf[c]
    pltpu.make_async_copy(o_buf.at[pl.ds(0, n_ctx - 1)], o_buf.at[pl.ds(0, n_ctx - 1)], e_sem.at[1]).wait()

    def out_copy(q):
        part = pl.ds(q * CHUNK, CHUNK)
        return pltpu.make_async_copy(out_buf.at[part], out_hbm.at[part], out_sem.at[q])

    for q in range(chunks):
        part = slice(q * CHUNK, (q + 1) * CHUNK)
        square = jnp.zeros((CHUNK, WIDE), F32)
        for j in range(tiles):
            wide = slice(j * WIDE, (j + 1) * WIDE)
            gated = a_buf[part, wide] + b_buf[part, wide] * dot(sc_buf[q, :, CHUNK : CHUNK + STATE], ent[:, wide])
            g_buf[:, wide] = gated
            square = square + gated * gated
        scale = lax.rsqrt(jnp.sum(square, axis=1, keepdims=True) * (1.0 / channels) + 1e-5)
        for j in range(tiles):
            wide = slice(j * WIDE, (j + 1) * WIDE)
            out_buf[part, wide] = (g_buf[:, wide] * scale * gain_ref[:, wide]).astype(BF16)
        out_copy(q).start()

    pltpu.make_async_copy(others, others, bc_sem.at[0]).wait()

    @pl.when(h == last_head)
    def _():
        sent = bc_buf.at[pl.ds(0, n_head * HALO)]
        pltpu.make_async_copy(sent, sent, hb_sem.at[0]).wait()

    halo_x.wait_send()
    for buffer, sem in ((d_buf, d_sem), (f_buf, f_sem), (o_buf, e_sem)):
        sent = buffer.at[pl.ds(0, n_ctx - 1)]
        pltpu.make_async_copy(sent, sent, sem.at[0]).wait()
    for q in range(chunks):
        out_copy(q).wait()


def per_device(
    n_ctx, n_head, x_in, bc_in, z_in, dt, log_decay, x_kernel, bc_kernel, x_bias, bc_bias, skip, norm_gain
):
    tokens, channels = x_in.shape
    heads = channels // HEAD_DIM
    chunks = tokens // CHUNK
    height = STATE * channels // n_ctx // 128
    anywhere, vmem = pl.BlockSpec(memory_space=pl.ANY), pl.BlockSpec(memory_space=pltpu.VMEM)
    dma = pltpu.SemaphoreType.DMA
    return pl.pallas_call(
        functools.partial(kernel, (n_ctx, n_head, tokens, channels)),
        out_shape=jax.ShapeDtypeStruct((tokens, channels), BF16),
        in_specs=[anywhere] * 3 + [vmem] * 8,
        out_specs=anywhere,
        scratch_shapes=[
            pltpu.VMEM((tokens + HALO, channels), BF16),
            pltpu.VMEM((tokens, channels), BF16),
            pltpu.VMEM((chunks, CHUNK + STATE, channels), BF16),
            pltpu.VMEM((tokens, channels), BF16),
            pltpu.VMEM((tokens, channels), F32),
            pltpu.VMEM((tokens, channels), F32),
            pltpu.VMEM((CHUNK, channels), F32),
            pltpu.VMEM((tokens, channels), BF16),
            pltpu.VMEM((2 * heads, channels), BF16),
            pltpu.VMEM((24, channels), F32),
            pltpu.VMEM((chunks, 2 * heads, CHUNK), BF16),
            pltpu.VMEM((chunks, 2 * heads, CHUNK), BF16),
            pltpu.VMEM((chunks, 2 * heads, CHUNK), BF16),
            pltpu.VMEM((tokens + HALO, 2, STATE), BF16),
            pltpu.VMEM((2 * (tokens + HALO), STATE), F32),
            pltpu.VMEM((chunks, STATE, CHUNK), BF16),
            pltpu.VMEM((chunks, CHUNK, CHUNK + STATE), BF16),
            pltpu.VMEM((n_ctx, height, 128), BF16),
            pltpu.VMEM((n_ctx, height, 128), BF16),
            pltpu.VMEM((n_ctx, height, 128), BF16),
            pltpu.VMEM((STATE, channels), BF16),
            pltpu.VMEM((1, 128), F32),
            pltpu.VMEM((n_ctx, 1, 128), F32),
            pltpu.VMEM((n_ctx, 128), F32),
            dma((chunks,)), dma, dma((chunks,)), dma((3,)), dma((2,)), dma((2,)), dma((2,)), dma((2,)), dma((2,)),
        ],
        compiler_params=pltpu.CompilerParams(
            collective_id=0, has_side_effects=True, vmem_limit_bytes=60 * 1024 * 1024
        ),
        cost_estimate=pl.CostEstimate(flops=2_500_000_000, bytes_accessed=14_000_000, transcendentals=5_000_000),
    )(
        x_in, bc_in, z_in, dt.T, log_decay.T, x_kernel, bc_kernel, x_bias[None], bc_bias, skip[None], norm_gain[None]
    )


def solution(mesh):
    placed = (
        P("ctx", "head"),
        P(("ctx", "head"), None, None),
        P("ctx", "head"),
        P("ctx", "head"),
        P("ctx", "head"),
        P(None, "head"),
        P(None, None, "head"),
        P("head"),
        P(None, "head"),
        P("head"),
        P("head"),
    )
    return jax.shard_map(
        functools.partial(per_device, mesh.shape["ctx"], mesh.shape["head"]),
        mesh=mesh, in_specs=placed, out_specs=P("ctx", "head"), check_vma=False,
    )
```

```python
import functools

import jax
import jax.numpy as jnp
from jax import lax
from jax.experimental import pallas as pl
from jax.experimental.pallas import tpu as pltpu
from jax.sharding import PartitionSpec as P

MESH = pl.DeviceIdType.MESH
F32, BF16 = jnp.float32, jnp.bfloat16
HEAD_DIM = 64
STATE = 128
CHUNK = 128
HALO = 16
WIDE = 256
HIGHEST = lax.Precision.HIGHEST


def split(value):
    high = value.astype(BF16)
    low = (value - high.astype(F32)).astype(BF16)
    return jnp.concatenate([high, low], axis=0)


def split_columns(value):
    high = value.astype(BF16).astype(F32)
    return jnp.concatenate([high, value - high], axis=0).T.astype(BF16)


def across(left, right):
    return lax.dot_general(left, right, (((0,), (0,)), ((), ())), preferred_element_type=F32)


def dot(left, right):
    return jnp.dot(left, right, preferred_element_type=F32)


def swish_of_twice(half):
    return half + half * jnp.tanh(half)


def kernel(
    sizes,
    x_hbm, bc_hbm, z_hbm, dt_ref, decay_ref, xk_ref, bck_ref, xb_ref, bcb_ref, skip_ref,
    a_buf, b_buf, c_buf, ent,
    x_buf, xc_buf, xs_buf, z_buf,
    spread, rows, w_t, g_t, full_t, shift, bc_buf, bc_f32, b_t, sc_buf,
    f_buf, r_buf, o_buf, d_send, d_buf, e_decay,
    x_sem, z_sem, bc_sem, hx_sem, hb_sem, d_sem, f_sem, e_sem,
):
    n_ctx, n_head, tokens, channels = sizes
    chunks, tiles = tokens // CHUNK, channels // WIDE
    heads = channels // HEAD_DIM
    share = tokens // n_head
    c, h = lax.axis_index("ctx"), lax.axis_index("head")
    following, preceding = lax.rem(c + 1, n_ctx), lax.rem(c + n_ctx - 1, n_ctx)
    last_head = n_head - 1

    barrier = pltpu.get_barrier_semaphore()

    @pl.loop(1, n_head)
    def _(d):
        pl.semaphore_signal(barrier, inc=1, device_id=(c, lax.rem(h + d, n_head)), device_id_type=MESH)

    @pl.when(h != last_head)
    def _():
        pl.semaphore_signal(barrier, inc=1, device_id=(preceding, last_head), device_id_type=MESH)

    @pl.loop(1, n_ctx)
    def _(d):
        pl.semaphore_signal(barrier, inc=1, device_id=(lax.rem(c + d, n_ctx), h), device_id_type=MESH)

    def x_copy(q):
        part = pl.ds(q * CHUNK, CHUNK)
        return pltpu.make_async_copy(
            x_hbm.at[part], x_buf.at[pl.ds(HALO + q * CHUNK, CHUNK)], x_sem.at[q]
        )

    for q in range(chunks):
        x_copy(q).start()
    z_copy = pltpu.make_async_copy(z_hbm, z_buf, z_sem)
    z_copy.start()

    d_send[...] = jnp.zeros_like(d_send)
    sums = lax.dot_general(
        jnp.ones((8, tokens), F32), decay_ref[...], (((1,), (1,)), ((), ())),
        precision=HIGHEST, preferred_element_type=F32,
    )
    d_send[:, 0:heads] = sums[0:1]
    d_buf[c] = d_send[...]

    pl.semaphore_wait(barrier, n_ctx - 1 + n_head - 1 + jnp.where(h == last_head, n_head - 1, 0))

    def columns(t):
        return pl.ds(pl.multiple_of(t * STATE, STATE), STATE)

    mine = bc_buf.at[pl.ds(HALO + h * share, share)]

    @pl.loop(1, n_head)
    def _(d):
        t = lax.rem(h + d, n_head)
        pltpu.make_async_remote_copy(
            src_ref=bc_hbm.at[:, :, columns(t)], dst_ref=mine, send_sem=bc_sem.at[0], recv_sem=bc_sem.at[1],
            device_id=(c, t), device_id_type=MESH,
        ).start()

    own_bc = pltpu.make_async_copy(bc_hbm.at[:, :, columns(h)], mine, bc_sem.at[2])
    own_bc.start()

    @pl.when(h == last_head)
    def _():
        @pl.loop(0, n_head)
        def _(t):
            pltpu.make_async_remote_copy(
                src_ref=bc_hbm.at[pl.ds(share - HALO, HALO), :, columns(t)], dst_ref=bc_buf.at[pl.ds(0, HALO)],
                send_sem=hb_sem.at[0], recv_sem=hb_sem.at[1], device_id=(following, t), device_id_type=MESH,
            ).start()

    halo_x = pltpu.make_async_remote_copy(
        src_ref=x_hbm.at[pl.ds(tokens - HALO, HALO)], dst_ref=x_buf.at[pl.ds(0, HALO)],
        send_sem=hx_sem.at[0], recv_sem=hx_sem.at[1], device_id=(following, h), device_id_type=MESH,
    )
    halo_x.start()

    @pl.loop(1, n_ctx)
    def _(d):
        pltpu.make_async_remote_copy(
            src_ref=d_send, dst_ref=d_buf.at[c], send_sem=d_sem.at[0], recv_sem=d_sem.at[1],
            device_id=(lax.rem(c + d, n_ctx), h), device_id_type=MESH,
        ).start()

    head_of = lax.broadcasted_iota(jnp.int32, (2 * heads, channels), 1) // HEAD_DIM
    row_of = lax.rem(lax.broadcasted_iota(jnp.int32, (2 * heads, channels), 0), heads)
    spread[...] = (head_of == row_of).astype(F32).astype(BF16)

    upto = (
        lax.broadcasted_iota(jnp.int32, (CHUNK, CHUNK), 0) <= lax.broadcasted_iota(jnp.int32, (CHUNK, CHUNK), 1)
    ).astype(F32)
    before = jnp.zeros((heads, 1), F32)
    to_middle, to_end = [], []
    for q in range(chunks):
        part = slice(q * CHUNK, (q + 1) * CHUNK)
        cum = jnp.dot(decay_ref[:, part], upto, precision=HIGHEST, preferred_element_type=F32)
        middle, last = cum[:, CHUNK // 2 - 1 : CHUNK // 2], cum[:, CHUNK - 1 : CHUNK]
        w_t[q] = split_columns(jnp.exp(middle - cum) * dt_ref[:, part])
        g_t[q] = split_columns(jnp.exp(cum - middle))
        full_t[q] = split_columns(jnp.exp(before + cum))
        to_middle.append(jnp.exp(middle))
        to_end.append(jnp.exp(last - middle))
        before = before + last
    lane = lax.broadcasted_iota(jnp.int32, (heads, 128), 1)
    packed = jnp.zeros((heads, 128), F32)
    for i, value in enumerate(to_middle + to_end):
        packed = jnp.where(lane == i, value, packed)
    eye = lax.broadcasted_iota(jnp.int32, (heads, heads), 0) == lax.broadcasted_iota(jnp.int32, (heads, heads), 1)
    skip_column = jnp.sum(jnp.where(eye, skip_ref[...], 0.0), axis=1, keepdims=True)
    packed = split(jnp.where(lane == 2 * chunks, skip_column, packed))
    for j in range(tiles):
        wide = slice(j * WIDE, (j + 1) * WIDE)
        rows[:, wide] = across(packed, spread[:, wide])[0 : rows.shape[0]]

    row = lax.broadcasted_iota(jnp.int32, shift.shape, 0)
    column = lax.broadcasted_iota(jnp.int32, shift.shape, 1)
    shift[...] = (column == lax.rem(row, CHUNK) + row // CHUNK + HALO - 3).astype(F32).astype(BF16)

    halo_x.wait_recv()

    @pl.when(c == 0)
    def _():
        x_buf[0:HALO] = jnp.zeros((HALO, channels), BF16)

    @pl.loop(0, chunks)
    def _(q):
        x_copy(q).wait()
        part = pl.ds(pl.multiple_of(q * CHUNK, CHUNK), CHUNK)
        around = pl.ds(pl.multiple_of(q * CHUNK, CHUNK), CHUNK + HALO)
        for j in range(tiles):
            wide = slice(j * WIDE, (j + 1) * WIDE)
            seen = x_buf[around, wide]
            moved = dot(shift[...], seen)
            half = 0.5 * xb_ref[:, wide] + (0.5 * xk_ref[3:4, wide]) * seen[HALO:].astype(F32)
            for tap in range(3):
                half = half + (0.5 * xk_ref[tap : tap + 1, wide]) * moved[tap * CHUNK : (tap + 1) * CHUNK]
            xc = swish_of_twice(half)
            xc_buf[part, wide] = xc.astype(BF16)
            xs_buf[q, 0:CHUNK, wide] = (xc * dot(w_t[q], spread[:, wide])).astype(BF16)

    others = bc_buf.at[pl.ds(0, tokens - share)]
    pltpu.make_async_copy(others, others, bc_sem.at[1]).wait()
    own_bc.wait()
    pltpu.make_async_copy(bc_buf.at[pl.ds(0, HALO)], bc_buf.at[pl.ds(0, HALO)], hb_sem.at[1]).wait()
    flat = bc_buf.reshape(2 * (tokens + HALO), STATE)
    bc_f32[0 : 2 * HALO] = jnp.where(c == 0, 0.0, flat[0 : 2 * HALO].astype(F32))
    causal = lax.broadcasted_iota(jnp.int32, (CHUNK, CHUNK), 0) >= lax.broadcasted_iota(jnp.int32, (CHUNK, CHUNK), 1)
    for q in range(chunks):
        first = 2 * (HALO + q * CHUNK)
        bc_f32[first : first + 2 * CHUNK] = flat[first : first + 2 * CHUNK].astype(F32)
        done = []
        for which in range(2):
            half = 0.5 * bcb_ref[which : which + 1]
            for tap in range(4):
                start = 2 * (HALO + q * CHUNK - 3 + tap) + which
                half = half + (0.5 * bck_ref[tap, which : which + 1]) * bc_f32[pl.ds(start, CHUNK, stride=2), :]
            done.append(swish_of_twice(half))
        b_t[q] = done[0].T.astype(BF16)
        b_part, c_part = done[0].astype(BF16), done[1].astype(BF16)
        scores = lax.dot_general(c_part, b_part, (((1,), (1,)), ((), ())), preferred_element_type=F32)
        sc_buf[q, :, 0:CHUNK] = jnp.where(causal, scores, 0.0).astype(BF16)
        sc_buf[q, :, CHUNK : CHUNK + STATE] = c_part
        c_buf[q * CHUNK : (q + 1) * CHUNK] = c_part

    def to_owner(k):
        return pltpu.make_async_remote_copy(
            src_ref=f_buf.at[k], dst_ref=r_buf.at[c], send_sem=f_sem.at[0], recv_sem=f_sem.at[1],
            device_id=(k, h), device_id_type=MESH,
        )

    per_tile = n_ctx // tiles
    deep = STATE * 128 // (STATE * channels // n_ctx)
    height = STATE // deep

    @pl.loop(0, tiles)
    def _(i):
        j = lax.rem(i + c // per_tile, tiles)
        wide = pl.ds(pl.multiple_of(j * WIDE, WIDE), WIDE)
        state = jnp.zeros((STATE, WIDE), F32)
        for q in range(chunks):
            scaled = state * rows[q : q + 1, wide]
            xs_buf[q, CHUNK : CHUNK + STATE, wide] = scaled.astype(BF16)
            fresh = dot(b_t[q], xs_buf[q, 0:CHUNK, wide])
            state = (scaled + fresh) * rows[chunks + q : chunks + q + 1, wide]
        for a in range(WIDE // 128):
            for b in range(deep):
                f_buf[j * per_tile + a * deep + b] = state[
                    b * height : (b + 1) * height, a * 128 : (a + 1) * 128
                ].astype(BF16)
        for s in range(per_tile):
            k = j * per_tile + s

            @pl.when(k != c)
            def _():
                to_owner(k).start()

    r_buf[c] = f_buf[c]
    z_copy.wait()

    def gate(first, end):
        @pl.loop(first, end)
        def _(q):
            part = pl.ds(pl.multiple_of(q * CHUNK, CHUNK), CHUNK)
            for j in range(tiles):
                wide = slice(j * WIDE, (j + 1) * WIDE)
                y = dot(sc_buf[q], xs_buf[q, :, wide]) * dot(g_t[q], spread[:, wide])
                y = y + rows[2 * chunks : 2 * chunks + 1, wide] * xc_buf[part, wide].astype(F32)
                swish = swish_of_twice(0.5 * z_buf[part, wide].astype(F32))
                a_buf[part, wide] = y * swish
                b_buf[part, wide] = dot(full_t[q], spread[:, wide]) * swish

    gate(0, chunks // 2)

    pltpu.make_async_copy(d_buf.at[pl.ds(0, n_ctx - 1)], d_buf.at[pl.ds(0, n_ctx - 1)], d_sem.at[1]).wait()
    pair = c // deep
    pick = (
        lax.broadcasted_iota(jnp.int32, (128, 128), 0)
        == 2 * pair + lax.broadcasted_iota(jnp.int32, (128, 128), 1) // HEAD_DIM
    ).astype(F32)
    totals = d_buf[...].reshape(n_ctx, 128)
    e_decay[...] = jnp.exp(jnp.dot(totals, pick, precision=HIGHEST, preferred_element_type=F32))
    pltpu.make_async_copy(r_buf.at[pl.ds(0, n_ctx - 1)], r_buf.at[pl.ds(0, n_ctx - 1)], f_sem.at[1]).wait()

    def advance(i, state):
        o_buf[i] = state.astype(BF16)
        return state * e_decay[pl.ds(i, 1), :] + r_buf[i].astype(F32)

    lax.fori_loop(0, n_ctx, advance, jnp.zeros((height, 128), F32))

    place = (
        pl.ds(pl.multiple_of(lax.rem(c, deep) * height, height), height),
        pl.ds(pl.multiple_of(pair * 128, 128), 128),
    )

    @pl.loop(1, n_ctx)
    def _(d):
        t = lax.rem(c + d, n_ctx)
        pltpu.make_async_remote_copy(
            src_ref=o_buf.at[t], dst_ref=ent.at[place], send_sem=e_sem.at[0], recv_sem=e_sem.at[1],
            device_id=(t, h), device_id_type=MESH,
        ).start()

    ent[place] = o_buf[c]
    gate(chunks // 2, chunks)
    pltpu.make_async_copy(o_buf.at[pl.ds(0, n_ctx - 1)], o_buf.at[pl.ds(0, n_ctx - 1)], e_sem.at[1]).wait()

    pltpu.make_async_copy(others, others, bc_sem.at[0]).wait()

    @pl.when(h == last_head)
    def _():
        sent = bc_buf.at[pl.ds(0, n_head * HALO)]
        pltpu.make_async_copy(sent, sent, hb_sem.at[0]).wait()

    halo_x.wait_send()
    for buffer, sem in ((d_buf, d_sem), (f_buf, f_sem), (o_buf, e_sem)):
        sent = buffer.at[pl.ds(0, n_ctx - 1)]
        pltpu.make_async_copy(sent, sent, sem.at[0]).wait()


def finish(a_ref, b_ref, c_ref, ent_ref, gain_ref, out_hbm, g_buf, out_buf, out_sem):
    tokens, channels = a_ref.shape
    chunks, tiles = tokens // CHUNK, channels // WIDE

    def out_copy(q):
        part = pl.ds(pl.multiple_of(q * CHUNK, CHUNK), CHUNK)
        return pltpu.make_async_copy(out_buf.at[part], out_hbm.at[part], out_sem.at[q])

    @pl.loop(0, chunks)
    def _(q):
        part = pl.ds(pl.multiple_of(q * CHUNK, CHUNK), CHUNK)
        square = jnp.zeros((CHUNK, WIDE), F32)
        for j in range(tiles):
            wide = slice(j * WIDE, (j + 1) * WIDE)
            gated = a_ref[part, wide] + b_ref[part, wide] * dot(c_ref[part], ent_ref[:, wide])
            g_buf[:, wide] = gated
            square = square + gated * gated
        scale = lax.rsqrt(jnp.sum(square, axis=1, keepdims=True) * (1.0 / channels) + 1e-5)
        for j in range(tiles):
            wide = slice(j * WIDE, (j + 1) * WIDE)
            out_buf[part, wide] = (g_buf[:, wide] * scale * gain_ref[:, wide]).astype(BF16)
        out_copy(q).start()

    @pl.loop(0, chunks)
    def _(q):
        out_copy(q).wait()


def per_device(
    n_ctx, n_head, x_in, bc_in, z_in, dt, log_decay, x_kernel, bc_kernel, x_bias, bc_bias, skip, norm_gain
):
    tokens, channels = x_in.shape
    heads = channels // HEAD_DIM
    chunks = tokens // CHUNK
    height = STATE * channels // n_ctx // 128
    anywhere, vmem = pl.BlockSpec(memory_space=pl.ANY), pl.BlockSpec(memory_space=pltpu.VMEM)
    dma = pltpu.SemaphoreType.DMA
    a, b, c_part, ent = pl.pallas_call(
        functools.partial(kernel, (n_ctx, n_head, tokens, channels)),
        out_shape=[
            pltpu.VMEM((tokens, channels), F32),
            pltpu.VMEM((tokens, channels), F32),
            pltpu.VMEM((tokens, STATE), BF16),
            pltpu.VMEM((STATE, channels), BF16),
        ],
        in_specs=[anywhere] * 3 + [vmem] * 7,
        out_specs=[vmem] * 4,
        scratch_shapes=[
            pltpu.VMEM((tokens + HALO, channels), BF16),
            pltpu.VMEM((tokens, channels), BF16),
            pltpu.VMEM((chunks, CHUNK + STATE, channels), BF16),
            pltpu.VMEM((tokens, channels), BF16),
            pltpu.VMEM((2 * heads, channels), BF16),
            pltpu.VMEM((24, channels), F32),
            pltpu.VMEM((chunks, CHUNK, 2 * heads), BF16),
            pltpu.VMEM((chunks, CHUNK, 2 * heads), BF16),
            pltpu.VMEM((chunks, CHUNK, 2 * heads), BF16),
            pltpu.VMEM((3 * CHUNK, CHUNK + HALO), BF16),
            pltpu.VMEM((tokens + HALO, 2, STATE), BF16),
            pltpu.VMEM((2 * (tokens + HALO), STATE), F32),
            pltpu.VMEM((chunks, STATE, CHUNK), BF16),
            pltpu.VMEM((chunks, CHUNK, CHUNK + STATE), BF16),
            pltpu.VMEM((n_ctx, height, 128), BF16),
            pltpu.VMEM((n_ctx, height, 128), BF16),
            pltpu.VMEM((n_ctx, height, 128), BF16),
            pltpu.VMEM((1, 128), F32),
            pltpu.VMEM((n_ctx, 1, 128), F32),
            pltpu.VMEM((n_ctx, 128), F32),
            dma((chunks,)), dma, dma((3,)), dma((2,)), dma((2,)), dma((2,)), dma((2,)), dma((2,)),
        ],
        compiler_params=pltpu.CompilerParams(
            collective_id=0, has_side_effects=True, vmem_limit_bytes=45_900_000
        ),
        cost_estimate=pl.CostEstimate(flops=2_500_000_000, bytes_accessed=10_000_000, transcendentals=5_000_000),
    )(x_in, bc_in, z_in, dt.T, log_decay.T, x_kernel, bc_kernel, x_bias[None], bc_bias, skip[None])
    return pl.pallas_call(
        finish,
        out_shape=jax.ShapeDtypeStruct((tokens, channels), BF16),
        in_specs=[vmem] * 5,
        out_specs=anywhere,
        scratch_shapes=[
            pltpu.VMEM((CHUNK, channels), F32),
            pltpu.VMEM((tokens, channels), BF16),
            dma((chunks,)),
        ],
        compiler_params=pltpu.CompilerParams(vmem_limit_bytes=16 * 1024 * 1024),
        cost_estimate=pl.CostEstimate(flops=600_000_000, bytes_accessed=4_000_000, transcendentals=1_000),
    )(a, b, c_part, ent, norm_gain[None])


def solution(mesh):
    placed = (
        P("ctx", "head"),
        P(("ctx", "head"), None, None),
        P("ctx", "head"),
        P("ctx", "head"),
        P("ctx", "head"),
        P(None, "head"),
        P(None, None, "head"),
        P("head"),
        P(None, "head"),
        P("head"),
        P("head"),
    )
    return jax.shard_map(
        functools.partial(per_device, mesh.shape["ctx"], mesh.shape["head"]),
        mesh=mesh, in_specs=placed, out_specs=P("ctx", "head"), check_vma=False,
    )
```

```python
import functools

import jax
import jax.numpy as jnp
from jax import lax
from jax.experimental import pallas as pl
from jax.experimental.pallas import tpu as pltpu
from jax.sharding import PartitionSpec as P

MESH = pl.DeviceIdType.MESH
F32, BF16 = jnp.float32, jnp.bfloat16
HEAD_DIM = 64
STATE = 128
CHUNK = 128
HALO = 16
WIDE = 256
PARTS = 2
HIGHEST = lax.Precision.HIGHEST


def split(value):
    high = value.astype(BF16)
    low = (value - high.astype(F32)).astype(BF16)
    return jnp.concatenate([high, low], axis=0)


def split_columns(value):
    high = value.astype(BF16).astype(F32)
    return jnp.concatenate([high, value - high], axis=0).T.astype(BF16)


def across(left, right):
    return lax.dot_general(left, right, (((0,), (0,)), ((), ())), preferred_element_type=F32)


def dot(left, right):
    return jnp.dot(left, right, preferred_element_type=F32)


def swish_of_twice(half):
    return half + half * jnp.tanh(half)


def kernel(
    sizes,
    x_hbm, bc_hbm, z_hbm, dt_ref, decay_ref, xk_ref, bck_ref, xb_ref, bcb_ref, skip_ref,
    a_buf, b_buf, c_buf, ent,
    x_buf, xc_buf, xs_buf, z_buf,
    spread, rows, w_t, g_t, full_t, shift, bc_raw, bc_f32, bc_send, bc_buf, b_conv, b_t, sc_buf,
    f_buf, r_buf, o_buf, d_send, d_buf, e_decay,
    x_sem, z_sem, raw_sem, bc_sem, hx_sem, hb_sem, d_sem, f_sem, e_sem,
):
    n_ctx, n_head, tokens, channels = sizes
    chunks, tiles = tokens // CHUNK, channels // WIDE
    heads = channels // HEAD_DIM
    share = tokens // n_head
    c, h = lax.axis_index("ctx"), lax.axis_index("head")
    following, preceding = lax.rem(c + 1, n_ctx), lax.rem(c + n_ctx - 1, n_ctx)
    last_head = n_head - 1

    barrier = pltpu.get_barrier_semaphore()

    @pl.loop(1, n_head)
    def _(d):
        pl.semaphore_signal(barrier, inc=1, device_id=(c, lax.rem(h + d, n_head)), device_id_type=MESH)

    @pl.when(h != last_head)
    def _():
        pl.semaphore_signal(barrier, inc=1, device_id=(preceding, last_head), device_id_type=MESH)

    @pl.loop(1, n_ctx)
    def _(d):
        pl.semaphore_signal(barrier, inc=1, device_id=(lax.rem(c + d, n_ctx), h), device_id_type=MESH)

    def columns(t):
        return pl.ds(pl.multiple_of(t * STATE, STATE), STATE)

    def raw_copy(t):
        return pltpu.make_async_copy(
            bc_hbm.at[:, :, t * STATE : (t + 1) * STATE], bc_raw.at[pl.ds(t * share, share)], raw_sem.at[t]
        )

    def x_copy(q):
        part = pl.ds(q * CHUNK, CHUNK)
        return pltpu.make_async_copy(
            x_hbm.at[part], x_buf.at[pl.ds(HALO + q * CHUNK, CHUNK)], x_sem.at[q]
        )

    for t in range(n_head):
        raw_copy(t).start()
    for q in range(chunks):
        x_copy(q).start()
    z_copy = pltpu.make_async_copy(z_hbm, z_buf, z_sem)
    z_copy.start()

    d_send[...] = jnp.zeros_like(d_send)
    sums = lax.dot_general(
        jnp.ones((8, tokens), F32), decay_ref[...], (((1,), (1,)), ((), ())),
        precision=HIGHEST, preferred_element_type=F32,
    )
    d_send[:, 0:heads] = sums[0:1]
    d_buf[c] = d_send[...]

    flat = bc_raw.reshape(2 * tokens, STATE)
    for t in range(n_head):
        raw_copy(t).wait()
        bc_f32[...] = flat[2 * t * share : 2 * (t + 1) * share].astype(F32)
        for which in range(2):
            bc_send[which, t] = bc_f32[pl.ds(which, share, stride=2), :].astype(BF16)

    head_of = lax.broadcasted_iota(jnp.int32, (2 * heads, channels), 1) // HEAD_DIM
    row_of = lax.rem(lax.broadcasted_iota(jnp.int32, (2 * heads, channels), 0), heads)
    spread[...] = (head_of == row_of).astype(F32).astype(BF16)

    upto = (
        lax.broadcasted_iota(jnp.int32, (CHUNK, CHUNK), 0) <= lax.broadcasted_iota(jnp.int32, (CHUNK, CHUNK), 1)
    ).astype(F32)
    before = jnp.zeros((heads, 1), F32)
    to_middle, to_end = [], []
    for q in range(chunks):
        part = slice(q * CHUNK, (q + 1) * CHUNK)
        cum = jnp.dot(decay_ref[:, part], upto, precision=HIGHEST, preferred_element_type=F32)
        middle, last = cum[:, CHUNK // 2 - 1 : CHUNK // 2], cum[:, CHUNK - 1 : CHUNK]
        w_t[q] = split_columns(jnp.exp(middle - cum) * dt_ref[:, part])
        g_t[q] = split_columns(jnp.exp(cum - middle))
        full_t[q] = split_columns(jnp.exp(before + cum))
        to_middle.append(jnp.exp(middle))
        to_end.append(jnp.exp(last - middle))
        before = before + last
    lane = lax.broadcasted_iota(jnp.int32, (heads, 128), 1)
    packed = jnp.zeros((heads, 128), F32)
    for i, value in enumerate(to_middle + to_end):
        packed = jnp.where(lane == i, value, packed)
    eye = lax.broadcasted_iota(jnp.int32, (heads, heads), 0) == lax.broadcasted_iota(jnp.int32, (heads, heads), 1)
    skip_column = jnp.sum(jnp.where(eye, skip_ref[...], 0.0), axis=1, keepdims=True)
    packed = split(jnp.where(lane == 2 * chunks, skip_column, packed))
    for j in range(tiles):
        wide = slice(j * WIDE, (j + 1) * WIDE)
        rows[:, wide] = across(packed, spread[:, wide])[0 : rows.shape[0]]

    row = lax.broadcasted_iota(jnp.int32, shift.shape, 0)
    column = lax.broadcasted_iota(jnp.int32, shift.shape, 1)
    shift[...] = (column == lax.rem(row, CHUNK) + row // CHUNK + HALO - 3).astype(F32).astype(BF16)

    pl.semaphore_wait(barrier, n_ctx - 1 + n_head - 1 + jnp.where(h == last_head, n_head - 1, 0))

    mine = pl.ds(pl.multiple_of(HALO + h * share, HALO), share)
    halo_x = pltpu.make_async_remote_copy(
        src_ref=x_hbm.at[pl.ds(tokens - HALO, HALO)], dst_ref=x_buf.at[pl.ds(0, HALO)],
        send_sem=hx_sem.at[0], recv_sem=hx_sem.at[1], device_id=(following, h), device_id_type=MESH,
    )

    for which in range(2):
        @pl.loop(1, n_head)
        def _(d):
            t = lax.rem(h + d, n_head)
            pltpu.make_async_remote_copy(
                src_ref=bc_send.at[which, t], dst_ref=bc_buf.at[which, mine],
                send_sem=bc_sem.at[2 * which], recv_sem=bc_sem.at[2 * which + 1],
                device_id=(c, t), device_id_type=MESH,
            ).start()

        @pl.when(h == last_head)
        def _():
            @pl.loop(0, n_head)
            def _(t):
                pltpu.make_async_remote_copy(
                    src_ref=bc_send.at[which, t, pl.ds(share - HALO, HALO)], dst_ref=bc_buf.at[which, pl.ds(0, HALO)],
                    send_sem=hb_sem.at[2 * which], recv_sem=hb_sem.at[2 * which + 1],
                    device_id=(following, t), device_id_type=MESH,
                ).start()

        if which == 0:
            halo_x.start()
        bc_buf[which, mine] = bc_send[which, h]

    @pl.loop(1, n_ctx)
    def _(d):
        pltpu.make_async_remote_copy(
            src_ref=d_send, dst_ref=d_buf.at[c], send_sem=d_sem.at[0], recv_sem=d_sem.at[1],
            device_id=(lax.rem(c + d, n_ctx), h), device_id_type=MESH,
        ).start()

    x_copy(0).wait()

    @pl.loop(0, chunks)
    def _(i):
        q = lax.rem(i + 1, chunks)

        @pl.when(q != 0)
        def _():
            x_copy(q).wait()

        @pl.when(q == 0)
        def _():
            halo_x.wait_recv()

            @pl.when(c == 0)
            def _():
                x_buf[0:HALO] = jnp.zeros((HALO, channels), BF16)

        part = pl.ds(pl.multiple_of(q * CHUNK, CHUNK), CHUNK)
        around = pl.ds(pl.multiple_of(q * CHUNK, CHUNK), CHUNK + HALO)
        for j in range(tiles):
            wide = slice(j * WIDE, (j + 1) * WIDE)
            seen = x_buf[around, wide]
            moved = dot(shift[...], seen)
            half = 0.5 * xb_ref[:, wide] + (0.5 * xk_ref[3:4, wide]) * seen[HALO:].astype(F32)
            for tap in range(3):
                half = half + (0.5 * xk_ref[tap : tap + 1, wide]) * moved[tap * CHUNK : (tap + 1) * CHUNK]
            xc = swish_of_twice(half)
            xc_buf[part, wide] = xc.astype(BF16)
            xs_buf[q, 0:CHUNK, wide] = (xc * dot(w_t[q], spread[:, wide])).astype(BF16)

    def others(which):
        return bc_buf.at[which, pl.ds(0, tokens - share)]

    def arrived(which):
        pltpu.make_async_copy(others(which), others(which), bc_sem.at[2 * which + 1]).wait()
        rim = bc_buf.at[which, pl.ds(0, HALO)]
        pltpu.make_async_copy(rim, rim, hb_sem.at[2 * which + 1]).wait()

        @pl.when(c == 0)
        def _():
            bc_buf[which, 0:HALO] = jnp.zeros((HALO, STATE), BF16)

    def convolved(which, q):
        seen = bc_buf[which, q * CHUNK : q * CHUNK + CHUNK + HALO]
        moved = dot(shift[...], seen)
        half = 0.5 * bcb_ref[which : which + 1] + (0.5 * bck_ref[3, which : which + 1]) * seen[HALO:].astype(F32)
        for tap in range(3):
            half = half + (0.5 * bck_ref[tap, which : which + 1]) * moved[tap * CHUNK : (tap + 1) * CHUNK]
        return swish_of_twice(half)

    arrived(0)
    for q in range(chunks):
        b_part = convolved(0, q)
        b_conv[q * CHUNK : (q + 1) * CHUNK] = b_part.astype(BF16)
        b_t[q] = b_part.T.astype(BF16)

    deep = n_ctx * 128 * PARTS // channels
    height = STATE // deep
    part_tiles = tiles // PARTS
    per_tile = n_ctx // part_tiles

    def to_owner(p, k):
        return pltpu.make_async_remote_copy(
            src_ref=f_buf.at[p, k], dst_ref=r_buf.at[p, c], send_sem=f_sem.at[2 * p], recv_sem=f_sem.at[2 * p + 1],
            device_id=(k, h), device_id_type=MESH,
        )

    for p in range(PARTS):
        @pl.loop(0, part_tiles)
        def _(i):
            j = lax.rem(i + c // per_tile, part_tiles)
            wide = pl.ds(pl.multiple_of((p * part_tiles + j) * WIDE, WIDE), WIDE)
            state = jnp.zeros((STATE, WIDE), F32)
            for q in range(chunks):
                scaled = state * rows[q : q + 1, wide]
                xs_buf[q, CHUNK : CHUNK + STATE, wide] = scaled.astype(BF16)
                fresh = dot(b_t[q], xs_buf[q, 0:CHUNK, wide])
                state = (scaled + fresh) * rows[chunks + q : chunks + q + 1, wide]
            for a in range(WIDE // 128):
                for b in range(deep):
                    f_buf[p, j * per_tile + a * deep + b] = state[
                        b * height : (b + 1) * height, a * 128 : (a + 1) * 128
                    ].astype(BF16)

            @pl.loop(0, per_tile)
            def _(s):
                k = j * per_tile + s

                @pl.when(k != c)
                def _():
                    to_owner(p, k).start()

        r_buf[p, c] = f_buf[p, c]

    arrived(1)
    causal = lax.broadcasted_iota(jnp.int32, (CHUNK, CHUNK), 0) >= lax.broadcasted_iota(jnp.int32, (CHUNK, CHUNK), 1)
    for q in range(chunks):
        b_part, c_part = b_conv[q * CHUNK : (q + 1) * CHUNK], convolved(1, q).astype(BF16)
        scores = lax.dot_general(c_part, b_part, (((1,), (1,)), ((), ())), preferred_element_type=F32)
        sc_buf[q, :, 0:CHUNK] = jnp.where(causal, scores, 0.0).astype(BF16)
        sc_buf[q, :, CHUNK : CHUNK + STATE] = c_part
        c_buf[q * CHUNK : (q + 1) * CHUNK] = c_part
    z_copy.wait()

    def gate(first, end):
        @pl.loop(first, end)
        def _(q):
            part = pl.ds(pl.multiple_of(q * CHUNK, CHUNK), CHUNK)
            for j in range(tiles):
                wide = slice(j * WIDE, (j + 1) * WIDE)
                y = dot(sc_buf[q], xs_buf[q, :, wide]) * dot(g_t[q], spread[:, wide])
                y = y + rows[2 * chunks : 2 * chunks + 1, wide] * xc_buf[part, wide].astype(F32)
                swish = swish_of_twice(0.5 * z_buf[part, wide].astype(F32))
                a_buf[part, wide] = y * swish
                b_buf[part, wide] = dot(full_t[q], spread[:, wide]) * swish

    pltpu.make_async_copy(d_buf.at[pl.ds(0, n_ctx - 1)], d_buf.at[pl.ds(0, n_ctx - 1)], d_sem.at[1]).wait()
    totals = d_buf[...].reshape(n_ctx, 128)

    def pair(p):
        return p * (channels // 128 // PARTS) + c // deep

    for p in range(PARTS):
        pick = (
            lax.broadcasted_iota(jnp.int32, (128, 128), 0)
            == 2 * pair(p) + lax.broadcasted_iota(jnp.int32, (128, 128), 1) // HEAD_DIM
        ).astype(F32)
        e_decay[p] = jnp.exp(jnp.dot(totals, pick, precision=HIGHEST, preferred_element_type=F32))

    def scan(p):
        pltpu.make_async_copy(
            r_buf.at[p, pl.ds(0, n_ctx - 1)], r_buf.at[p, pl.ds(0, n_ctx - 1)], f_sem.at[2 * p + 1]
        ).wait()

        state = jnp.zeros((height, 128), F32)
        for i in range(n_ctx):
            o_buf[p, i] = state.astype(BF16)
            state = state * e_decay[p, i : i + 1, :] + r_buf[p, i].astype(F32)

        place = (
            pl.ds(pl.multiple_of(lax.rem(c, deep) * height, height), height),
            pl.ds(pl.multiple_of(pair(p) * 128, 128), 128),
        )

        @pl.loop(1, n_ctx)
        def _(d):
            t = lax.rem(c + d, n_ctx)
            pltpu.make_async_remote_copy(
                src_ref=o_buf.at[p, t], dst_ref=ent.at[place], send_sem=e_sem.at[2 * p], recv_sem=e_sem.at[2 * p + 1],
                device_id=(t, h), device_id_type=MESH,
            ).start()

        ent[place] = o_buf[p, c]

    def entered(p):
        pltpu.make_async_copy(
            o_buf.at[p, pl.ds(0, n_ctx - 1)], o_buf.at[p, pl.ds(0, n_ctx - 1)], e_sem.at[2 * p + 1]
        ).wait()

    gate(0, chunks // 2)
    scan(0)
    gate(chunks // 2, chunks - 1)
    scan(1)
    gate(chunks - 1, chunks)

    entered(0)

    @pl.loop(0, chunks)
    def _(q):
        part = pl.ds(pl.multiple_of(q * CHUNK, CHUNK), CHUNK)
        for j in range(part_tiles):
            wide = slice(j * WIDE, (j + 1) * WIDE)
            a_buf[part, wide] = a_buf[part, wide] + b_buf[part, wide] * dot(c_buf[part], ent[:, wide])

    for p in range(1, PARTS):
        entered(p)

    for which in range(2):
        pltpu.make_async_copy(others(which), others(which), bc_sem.at[2 * which]).wait()

    @pl.when(h == last_head)
    def _():
        for which in range(2):
            sent = bc_buf.at[which, pl.ds(0, n_head * HALO)]
            pltpu.make_async_copy(sent, sent, hb_sem.at[2 * which]).wait()

    halo_x.wait_send()
    sent = d_buf.at[pl.ds(0, n_ctx - 1)]
    pltpu.make_async_copy(sent, sent, d_sem.at[0]).wait()
    for buffer, sem in ((f_buf, f_sem), (o_buf, e_sem)):
        for p in range(PARTS):
            sent = buffer.at[p, pl.ds(0, n_ctx - 1)]
            pltpu.make_async_copy(sent, sent, sem.at[2 * p]).wait()


def finish(a_ref, b_ref, c_ref, ent_ref, gain_ref, out_hbm, g_buf, out_buf, out_sem):
    tokens, channels = a_ref.shape
    chunks, tiles = tokens // CHUNK, channels // WIDE

    def out_copy(q):
        part = pl.ds(pl.multiple_of(q * CHUNK, CHUNK), CHUNK)
        return pltpu.make_async_copy(out_buf.at[part], out_hbm.at[part], out_sem.at[q])

    @pl.loop(0, chunks)
    def _(q):
        part = pl.ds(pl.multiple_of(q * CHUNK, CHUNK), CHUNK)
        square = jnp.zeros((CHUNK, WIDE), F32)
        for j in range(tiles):
            wide = slice(j * WIDE, (j + 1) * WIDE)
            gated = a_ref[part, wide]
            if j >= tiles // PARTS:
                gated = gated + b_ref[part, wide] * dot(c_ref[part], ent_ref[:, wide])
                g_buf[:, wide] = gated
            square = square + gated * gated
        scale = lax.rsqrt(jnp.sum(square, axis=1, keepdims=True) * (1.0 / channels) + 1e-5)
        for j in range(tiles):
            wide = slice(j * WIDE, (j + 1) * WIDE)
            gated = a_ref[part, wide] if j < tiles // PARTS else g_buf[:, wide]
            out_buf[part, wide] = (gated * scale * gain_ref[:, wide]).astype(BF16)
        out_copy(q).start()

    @pl.loop(0, chunks)
    def _(q):
        out_copy(q).wait()


def per_device(
    n_ctx, n_head, x_in, bc_in, z_in, dt, log_decay, x_kernel, bc_kernel, x_bias, bc_bias, skip, norm_gain
):
    tokens, channels = x_in.shape
    heads = channels // HEAD_DIM
    chunks = tokens // CHUNK
    height = STATE * channels // PARTS // n_ctx // 128
    share = tokens // n_head
    anywhere, vmem = pl.BlockSpec(memory_space=pl.ANY), pl.BlockSpec(memory_space=pltpu.VMEM)
    dma = pltpu.SemaphoreType.DMA
    a, b, c_part, ent = pl.pallas_call(
        functools.partial(kernel, (n_ctx, n_head, tokens, channels)),
        out_shape=[
            pltpu.VMEM((tokens, channels), F32),
            pltpu.VMEM((tokens, channels), F32),
            pltpu.VMEM((tokens, STATE), BF16),
            pltpu.VMEM((STATE, channels), BF16),
        ],
        in_specs=[anywhere] * 3 + [vmem] * 7,
        out_specs=[vmem] * 4,
        scratch_shapes=[
            pltpu.VMEM((tokens + HALO, channels), BF16),
            pltpu.VMEM((tokens, channels), BF16),
            pltpu.VMEM((chunks, CHUNK + STATE, channels), BF16),
            pltpu.VMEM((tokens, channels), BF16),
            pltpu.VMEM((2 * heads, channels), BF16),
            pltpu.VMEM((24, channels), F32),
            pltpu.VMEM((chunks, CHUNK, 2 * heads), BF16),
            pltpu.VMEM((chunks, CHUNK, 2 * heads), BF16),
            pltpu.VMEM((chunks, CHUNK, 2 * heads), BF16),
            pltpu.VMEM((3 * CHUNK, CHUNK + HALO), BF16),
            pltpu.VMEM((tokens, 2, STATE), BF16),
            pltpu.VMEM((2 * share, STATE), F32),
            pltpu.VMEM((2, n_head, share, STATE), BF16),
            pltpu.VMEM((2, tokens + HALO, STATE), BF16),
            pltpu.VMEM((tokens, STATE), BF16),
            pltpu.VMEM((chunks, STATE, CHUNK), BF16),
            pltpu.VMEM((chunks, CHUNK, CHUNK + STATE), BF16),
            pltpu.VMEM((PARTS, n_ctx, height, 128), BF16),
            pltpu.VMEM((PARTS, n_ctx, height, 128), BF16),
            pltpu.VMEM((PARTS, n_ctx, height, 128), BF16),
            pltpu.VMEM((1, 128), F32),
            pltpu.VMEM((n_ctx, 1, 128), F32),
            pltpu.VMEM((PARTS, n_ctx, 128), F32),
            dma((chunks,)), dma, dma((n_head,)), dma((4,)), dma((2,)), dma((4,)), dma((2,)),
            dma((2 * PARTS,)), dma((2 * PARTS,)),
        ],
        compiler_params=pltpu.CompilerParams(
            collective_id=0, has_side_effects=True, vmem_limit_bytes=45_900_000
        ),
        cost_estimate=pl.CostEstimate(flops=2_500_000_000, bytes_accessed=10_000_000, transcendentals=5_000_000),
    )(x_in, bc_in, z_in, dt.T, log_decay.T, x_kernel, bc_kernel, x_bias[None], bc_bias, skip[None])
    return pl.pallas_call(
        finish,
        out_shape=jax.ShapeDtypeStruct((tokens, channels), BF16),
        in_specs=[vmem] * 5,
        out_specs=anywhere,
        scratch_shapes=[
            pltpu.VMEM((CHUNK, channels), F32),
            pltpu.VMEM((tokens, channels), BF16),
            dma((chunks,)),
        ],
        compiler_params=pltpu.CompilerParams(vmem_limit_bytes=16 * 1024 * 1024),
        cost_estimate=pl.CostEstimate(flops=600_000_000, bytes_accessed=4_000_000, transcendentals=1_000),
    )(a, b, c_part, ent, norm_gain[None])


def solution(mesh):
    placed = (
        P("ctx", "head"),
        P(("ctx", "head"), None, None),
        P("ctx", "head"),
        P("ctx", "head"),
        P("ctx", "head"),
        P(None, "head"),
        P(None, None, "head"),
        P("head"),
        P(None, "head"),
        P("head"),
        P("head"),
    )
    return jax.shard_map(
        functools.partial(per_device, mesh.shape["ctx"], mesh.shape["head"]),
        mesh=mesh, in_specs=placed, out_specs=P("ctx", "head"), check_vma=False,
    )
```

```python
import functools

import jax
import jax.numpy as jnp
from jax import lax
from jax.experimental import pallas as pl
from jax.experimental.pallas import tpu as pltpu
from jax.sharding import PartitionSpec as P

MESH = pl.DeviceIdType.MESH
F32, BF16 = jnp.float32, jnp.bfloat16
HEAD_DIM = 64
STATE = 128
CHUNK = 128
HALO = 16
WIDE = 256
PARTS = 2
HIGHEST = lax.Precision.HIGHEST


def split(value):
    high = value.astype(BF16)
    low = (value - high.astype(F32)).astype(BF16)
    return jnp.concatenate([high, low], axis=0)


def split_columns(value):
    high = value.astype(BF16).astype(F32)
    return jnp.concatenate([high, value - high], axis=0).T.astype(BF16)


def across(left, right):
    return lax.dot_general(left, right, (((0,), (0,)), ((), ())), preferred_element_type=F32)


def dot(left, right):
    return jnp.dot(left, right, preferred_element_type=F32)


def swish_of_twice(half):
    return half + half * jnp.tanh(half)


def kernel(
    sizes,
    x_hbm, bc_hbm, z_hbm, dt_hbm, decay_hbm, xk_hbm, bck_hbm, xb_hbm, bcb_hbm, skip_hbm,
    a_buf, b_buf, c_buf, ent, square_buf,
    dt_ref, decay_ref, xk_ref, bck_ref, xb_ref, bcb_ref, skip_ref,
    x_buf, xc_buf, xs_buf, z_buf,
    spread, rows, w_t, g_t, full_t, shift, bc_raw, bc_f32, bc_send, bc_buf, b_conv, b_t, sc_buf,
    f_buf, r_buf, o_buf, d_send, d_buf, e_decay,
    small_sem, x_sem, z_sem, raw_sem, bc_sem, hx_sem, hb_sem, d_sem, f_sem, e_sem,
):
    n_ctx, n_head, tokens, channels = sizes
    chunks, tiles = tokens // CHUNK, channels // WIDE
    heads = channels // HEAD_DIM
    share = tokens // n_head
    c, h = lax.axis_index("ctx"), lax.axis_index("head")
    following, preceding = lax.rem(c + 1, n_ctx), lax.rem(c + n_ctx - 1, n_ctx)
    last_head = n_head - 1

    barrier = pltpu.get_barrier_semaphore()

    @pl.loop(1, n_head)
    def _(d):
        pl.semaphore_signal(barrier, inc=1, device_id=(c, lax.rem(h + d, n_head)), device_id_type=MESH)

    @pl.when(h != last_head)
    def _():
        pl.semaphore_signal(barrier, inc=1, device_id=(preceding, last_head), device_id_type=MESH)

    @pl.loop(1, n_ctx)
    def _(d):
        pl.semaphore_signal(barrier, inc=1, device_id=(lax.rem(c + d, n_ctx), h), device_id_type=MESH)

    def columns(t):
        return pl.ds(pl.multiple_of(t * STATE, STATE), STATE)

    def raw_copy(t):
        return pltpu.make_async_copy(
            bc_hbm.at[:, :, t * STATE : (t + 1) * STATE], bc_raw.at[pl.ds(t * share, share)], raw_sem.at[t]
        )

    def x_copy(q):
        part = pl.ds(q * CHUNK, CHUNK)
        return pltpu.make_async_copy(
            x_hbm.at[part], x_buf.at[pl.ds(HALO + q * CHUNK, CHUNK)], x_sem.at[q]
        )

    small = [
        pltpu.make_async_copy(source, target, small_sem.at[i])
        for i, (source, target) in enumerate((
            (decay_hbm, decay_ref), (dt_hbm, dt_ref), (skip_hbm, skip_ref), (xk_hbm, xk_ref), (xb_hbm, xb_ref),
            (bck_hbm, bck_ref), (bcb_hbm, bcb_ref),
        ))
    ]
    small[0].start()
    for t in range(n_head):
        raw_copy(t).start()
    for copy in small[1:]:
        copy.start()
    for q in range(chunks):
        x_copy(q).start()
    z_copy = pltpu.make_async_copy(z_hbm, z_buf, z_sem)
    z_copy.start()

    d_send[...] = jnp.zeros_like(d_send)
    small[0].wait()
    sums = lax.dot_general(
        jnp.ones((8, tokens), F32), decay_ref[...], (((1,), (1,)), ((), ())),
        precision=HIGHEST, preferred_element_type=F32,
    )
    d_send[:, 0:heads] = sums[0:1]
    d_buf[c] = d_send[...]

    flat = bc_raw.reshape(2 * tokens, STATE)
    for t in range(n_head):
        raw_copy(t).wait()
        bc_f32[...] = flat[2 * t * share : 2 * (t + 1) * share].astype(F32)
        for which in range(2):
            bc_send[which, t] = bc_f32[pl.ds(which, share, stride=2), :].astype(BF16)

    head_of = lax.broadcasted_iota(jnp.int32, (2 * heads, channels), 1) // HEAD_DIM
    row_of = lax.rem(lax.broadcasted_iota(jnp.int32, (2 * heads, channels), 0), heads)
    spread[...] = (head_of == row_of).astype(F32).astype(BF16)

    for copy in small[1:]:
        copy.wait()

    upto = (
        lax.broadcasted_iota(jnp.int32, (CHUNK, CHUNK), 0) <= lax.broadcasted_iota(jnp.int32, (CHUNK, CHUNK), 1)
    ).astype(F32)
    before = jnp.zeros((heads, 1), F32)
    to_middle, to_end = [], []
    for q in range(chunks):
        part = slice(q * CHUNK, (q + 1) * CHUNK)
        cum = jnp.dot(decay_ref[:, part], upto, precision=HIGHEST, preferred_element_type=F32)
        middle, last = cum[:, CHUNK // 2 - 1 : CHUNK // 2], cum[:, CHUNK - 1 : CHUNK]
        w_t[q] = split_columns(jnp.exp(middle - cum) * dt_ref[:, part])
        g_t[q] = split_columns(jnp.exp(cum - middle))
        full_t[q] = split_columns(jnp.exp(before + cum))
        to_middle.append(jnp.exp(middle))
        to_end.append(jnp.exp(last - middle))
        before = before + last
    lane = lax.broadcasted_iota(jnp.int32, (heads, 128), 1)
    packed = jnp.zeros((heads, 128), F32)
    for i, value in enumerate(to_middle + to_end):
        packed = jnp.where(lane == i, value, packed)
    eye = lax.broadcasted_iota(jnp.int32, (heads, heads), 0) == lax.broadcasted_iota(jnp.int32, (heads, heads), 1)
    skip_column = jnp.sum(jnp.where(eye, skip_ref[...], 0.0), axis=1, keepdims=True)
    packed = split(jnp.where(lane == 2 * chunks, skip_column, packed))
    for j in range(tiles):
        wide = slice(j * WIDE, (j + 1) * WIDE)
        rows[:, wide] = across(packed, spread[:, wide])[0 : rows.shape[0]]

    row = lax.broadcasted_iota(jnp.int32, shift.shape, 0)
    column = lax.broadcasted_iota(jnp.int32, shift.shape, 1)
    shift[...] = (column == lax.rem(row, CHUNK) + row // CHUNK + HALO - 3).astype(F32).astype(BF16)

    pl.semaphore_wait(barrier, n_ctx - 1 + n_head - 1 + jnp.where(h == last_head, n_head - 1, 0))

    mine = pl.ds(pl.multiple_of(HALO + h * share, HALO), share)
    halo_x = pltpu.make_async_remote_copy(
        src_ref=x_hbm.at[pl.ds(tokens - HALO, HALO)], dst_ref=x_buf.at[pl.ds(0, HALO)],
        send_sem=hx_sem.at[0], recv_sem=hx_sem.at[1], device_id=(following, h), device_id_type=MESH,
    )

    def share_out(which):
        @pl.loop(1, n_head)
        def _(d):
            t = lax.rem(h + d, n_head)
            pltpu.make_async_remote_copy(
                src_ref=bc_send.at[which, t], dst_ref=bc_buf.at[which, mine],
                send_sem=bc_sem.at[2 * which], recv_sem=bc_sem.at[2 * which + 1],
                device_id=(c, t), device_id_type=MESH,
            ).start()

        @pl.when(h == last_head)
        def _():
            @pl.loop(0, n_head)
            def _(t):
                pltpu.make_async_remote_copy(
                    src_ref=bc_send.at[which, t, pl.ds(share - HALO, HALO)], dst_ref=bc_buf.at[which, pl.ds(0, HALO)],
                    send_sem=hb_sem.at[2 * which], recv_sem=hb_sem.at[2 * which + 1],
                    device_id=(following, t), device_id_type=MESH,
                ).start()

        bc_buf[which, mine] = bc_send[which, h]

    share_out(0)
    halo_x.start()

    @pl.loop(1, n_ctx)
    def _(d):
        pltpu.make_async_remote_copy(
            src_ref=d_send, dst_ref=d_buf.at[c], send_sem=d_sem.at[0], recv_sem=d_sem.at[1],
            device_id=(lax.rem(c + d, n_ctx), h), device_id_type=MESH,
        ).start()

    x_copy(0).wait()

    @pl.loop(0, chunks)
    def _(i):
        q = lax.rem(i + 1, chunks)

        @pl.when(q != 0)
        def _():
            x_copy(q).wait()

        @pl.when(q == 0)
        def _():
            halo_x.wait_recv()

            @pl.when(c == 0)
            def _():
                x_buf[0:HALO] = jnp.zeros((HALO, channels), BF16)

        part = pl.ds(pl.multiple_of(q * CHUNK, CHUNK), CHUNK)
        around = pl.ds(pl.multiple_of(q * CHUNK, CHUNK), CHUNK + HALO)
        for j in range(tiles):
            wide = slice(j * WIDE, (j + 1) * WIDE)
            seen = x_buf[around, wide]
            moved = dot(shift[...], seen)
            half = 0.5 * xb_ref[:, wide] + (0.5 * xk_ref[3:4, wide]) * seen[HALO:].astype(F32)
            for tap in range(3):
                half = half + (0.5 * xk_ref[tap : tap + 1, wide]) * moved[tap * CHUNK : (tap + 1) * CHUNK]
            xc = swish_of_twice(half)
            xc_buf[part, wide] = xc.astype(BF16)
            xs_buf[q, 0:CHUNK, wide] = (xc * dot(w_t[q], spread[:, wide])).astype(BF16)

    def others(which):
        return bc_buf.at[which, pl.ds(0, tokens - share)]

    def arrived(which):
        pltpu.make_async_copy(others(which), others(which), bc_sem.at[2 * which + 1]).wait()
        rim = bc_buf.at[which, pl.ds(0, HALO)]
        pltpu.make_async_copy(rim, rim, hb_sem.at[2 * which + 1]).wait()

        @pl.when(c == 0)
        def _():
            bc_buf[which, 0:HALO] = jnp.zeros((HALO, STATE), BF16)

    def convolved(which, q):
        seen = bc_buf[which, q * CHUNK : q * CHUNK + CHUNK + HALO]
        moved = dot(shift[...], seen)
        half = 0.5 * bcb_ref[which : which + 1] + (0.5 * bck_ref[3, which : which + 1]) * seen[HALO:].astype(F32)
        for tap in range(3):
            half = half + (0.5 * bck_ref[tap, which : which + 1]) * moved[tap * CHUNK : (tap + 1) * CHUNK]
        return swish_of_twice(half)

    arrived(0)
    share_out(1)
    for q in range(chunks):
        b_part = convolved(0, q)
        b_conv[q * CHUNK : (q + 1) * CHUNK] = b_part.astype(BF16)
        b_t[q] = b_part.T.astype(BF16)

    deep = n_ctx * 128 * PARTS // channels
    height = STATE // deep
    part_tiles = tiles // PARTS
    per_tile = n_ctx // part_tiles

    def to_owner(p, k):
        return pltpu.make_async_remote_copy(
            src_ref=f_buf.at[p, k], dst_ref=r_buf.at[p, c], send_sem=f_sem.at[2 * p], recv_sem=f_sem.at[2 * p + 1],
            device_id=(k, h), device_id_type=MESH,
        )

    for p in range(PARTS):
        @pl.loop(0, part_tiles)
        def _(i):
            j = lax.rem(i + c // per_tile, part_tiles)
            wide = pl.ds(pl.multiple_of((p * part_tiles + j) * WIDE, WIDE), WIDE)
            state = jnp.zeros((STATE, WIDE), F32)
            for q in range(chunks):
                scaled = state * rows[q : q + 1, wide]
                xs_buf[q, CHUNK : CHUNK + STATE, wide] = scaled.astype(BF16)
                fresh = dot(b_t[q], xs_buf[q, 0:CHUNK, wide])
                state = (scaled + fresh) * rows[chunks + q : chunks + q + 1, wide]
            for a in range(WIDE // 128):
                for b in range(deep):
                    f_buf[p, j * per_tile + a * deep + b] = state[
                        b * height : (b + 1) * height, a * 128 : (a + 1) * 128
                    ].astype(BF16)

            @pl.loop(0, per_tile)
            def _(s):
                k = j * per_tile + s

                @pl.when(k != c)
                def _():
                    to_owner(p, k).start()

        r_buf[p, c] = f_buf[p, c]

    arrived(1)
    causal = lax.broadcasted_iota(jnp.int32, (CHUNK, CHUNK), 0) >= lax.broadcasted_iota(jnp.int32, (CHUNK, CHUNK), 1)
    for q in range(chunks):
        b_part, c_part = b_conv[q * CHUNK : (q + 1) * CHUNK], convolved(1, q).astype(BF16)
        scores = lax.dot_general(c_part, b_part, (((1,), (1,)), ((), ())), preferred_element_type=F32)
        sc_buf[q, :, 0:CHUNK] = jnp.where(causal, scores, 0.0).astype(BF16)
        sc_buf[q, :, CHUNK : CHUNK + STATE] = c_part
        c_buf[q * CHUNK : (q + 1) * CHUNK] = c_part
    z_copy.wait()

    def gate(first, end):
        @pl.loop(first, end)
        def _(q):
            part = pl.ds(pl.multiple_of(q * CHUNK, CHUNK), CHUNK)
            for j in range(tiles):
                wide = slice(j * WIDE, (j + 1) * WIDE)
                y = dot(sc_buf[q], xs_buf[q, :, wide]) * dot(g_t[q], spread[:, wide])
                y = y + rows[2 * chunks : 2 * chunks + 1, wide] * xc_buf[part, wide].astype(F32)
                swish = swish_of_twice(0.5 * z_buf[part, wide].astype(F32))
                a_buf[part, wide] = y * swish
                b_buf[part, wide] = dot(full_t[q], spread[:, wide]) * swish

    pltpu.make_async_copy(d_buf.at[pl.ds(0, n_ctx - 1)], d_buf.at[pl.ds(0, n_ctx - 1)], d_sem.at[1]).wait()
    totals = d_buf[...].reshape(n_ctx, 128)

    def pair(p):
        return p * (channels // 128 // PARTS) + c // deep

    for p in range(PARTS):
        pick = (
            lax.broadcasted_iota(jnp.int32, (128, 128), 0)
            == 2 * pair(p) + lax.broadcasted_iota(jnp.int32, (128, 128), 1) // HEAD_DIM
        ).astype(F32)
        e_decay[p] = jnp.exp(jnp.dot(totals, pick, precision=HIGHEST, preferred_element_type=F32))

    def scan(p):
        pltpu.make_async_copy(
            r_buf.at[p, pl.ds(0, n_ctx - 1)], r_buf.at[p, pl.ds(0, n_ctx - 1)], f_sem.at[2 * p + 1]
        ).wait()

        state = jnp.zeros((height, 128), F32)
        for i in range(n_ctx):
            o_buf[p, i] = state.astype(BF16)
            state = state * e_decay[p, i : i + 1, :] + r_buf[p, i].astype(F32)

        place = (
            pl.ds(pl.multiple_of(lax.rem(c, deep) * height, height), height),
            pl.ds(pl.multiple_of(pair(p) * 128, 128), 128),
        )

        @pl.loop(1, n_ctx)
        def _(d):
            t = lax.rem(c + d, n_ctx)
            pltpu.make_async_remote_copy(
                src_ref=o_buf.at[p, t], dst_ref=ent.at[place], send_sem=e_sem.at[2 * p], recv_sem=e_sem.at[2 * p + 1],
                device_id=(t, h), device_id_type=MESH,
            ).start()

        ent[place] = o_buf[p, c]

    def entered(p):
        pltpu.make_async_copy(
            o_buf.at[p, pl.ds(0, n_ctx - 1)], o_buf.at[p, pl.ds(0, n_ctx - 1)], e_sem.at[2 * p + 1]
        ).wait()

    gate(0, chunks // 2)
    scan(0)
    gate(chunks // 2, chunks - 1)
    scan(1)
    gate(chunks - 1, chunks)

    entered(0)

    @pl.loop(0, chunks)
    def _(q):
        part = pl.ds(pl.multiple_of(q * CHUNK, CHUNK), CHUNK)
        square = jnp.zeros((CHUNK, WIDE), F32)
        for j in range(part_tiles):
            wide = slice(j * WIDE, (j + 1) * WIDE)
            gated = a_buf[part, wide] + b_buf[part, wide] * dot(c_buf[part], ent[:, wide])
            a_buf[part, wide] = gated
            square = square + gated * gated
        square_buf[part] = square[:, : WIDE // 2] + square[:, WIDE // 2 :]

    for p in range(1, PARTS):
        entered(p)

    for which in range(2):
        pltpu.make_async_copy(others(which), others(which), bc_sem.at[2 * which]).wait()

    @pl.when(h == last_head)
    def _():
        for which in range(2):
            sent = bc_buf.at[which, pl.ds(0, n_head * HALO)]
            pltpu.make_async_copy(sent, sent, hb_sem.at[2 * which]).wait()

    halo_x.wait_send()
    sent = d_buf.at[pl.ds(0, n_ctx - 1)]
    pltpu.make_async_copy(sent, sent, d_sem.at[0]).wait()
    for buffer, sem in ((f_buf, f_sem), (o_buf, e_sem)):
        for p in range(PARTS):
            sent = buffer.at[p, pl.ds(0, n_ctx - 1)]
            pltpu.make_async_copy(sent, sent, sem.at[2 * p]).wait()


def finish(a_ref, b_ref, c_ref, ent_ref, square_ref, gain_ref, out_hbm, g_buf, out_buf, out_sem):
    tokens, channels = a_ref.shape
    chunks, tiles = tokens // CHUNK, channels // WIDE

    def out_copy(q):
        part = pl.ds(q * CHUNK, CHUNK)
        return pltpu.make_async_copy(out_buf.at[part], out_hbm.at[part], out_sem.at[q])

    first = tiles // PARTS * WIDE
    for q in range(chunks):
        part = slice(q * CHUNK, (q + 1) * CHUNK)
        square = square_ref[part]
        for j in range(tiles // PARTS, tiles):
            wide = slice(j * WIDE, (j + 1) * WIDE)
            gated = a_ref[part, wide] + b_ref[part, wide] * dot(c_ref[part], ent_ref[:, wide])
            g_buf[part, wide.start - first : wide.stop - first] = gated
            squared = gated * gated
            square = square + squared[:, : WIDE // 2] + squared[:, WIDE // 2 :]
        scale = lax.rsqrt(jnp.sum(square, axis=1, keepdims=True) * (1.0 / channels) + 1e-5)
        for j in range(tiles):
            wide = slice(j * WIDE, (j + 1) * WIDE)
            if j < tiles // PARTS:
                gated = a_ref[part, wide]
            else:
                gated = g_buf[part, wide.start - first : wide.stop - first]
            out_buf[part, wide] = (gated * scale * gain_ref[:, wide]).astype(BF16)
        out_copy(q).start()

    for q in range(chunks):
        out_copy(q).wait()


def per_device(
    n_ctx, n_head, x_in, bc_in, z_in, dt, log_decay, x_kernel, bc_kernel, x_bias, bc_bias, skip, norm_gain
):
    tokens, channels = x_in.shape
    heads = channels // HEAD_DIM
    chunks = tokens // CHUNK
    height = STATE * channels // PARTS // n_ctx // 128
    share = tokens // n_head
    anywhere, vmem = pl.BlockSpec(memory_space=pl.ANY), pl.BlockSpec(memory_space=pltpu.VMEM)
    dma = pltpu.SemaphoreType.DMA
    a, b, c_part, ent, square = pl.pallas_call(
        functools.partial(kernel, (n_ctx, n_head, tokens, channels)),
        out_shape=[
            pltpu.VMEM((tokens, channels), F32),
            pltpu.VMEM((tokens, channels), F32),
            pltpu.VMEM((tokens, STATE), BF16),
            pltpu.VMEM((STATE, channels), BF16),
            pltpu.VMEM((tokens, WIDE // 2), F32),
        ],
        in_specs=[anywhere] * 10,
        out_specs=[vmem] * 5,
        scratch_shapes=[
            pltpu.VMEM((heads, tokens), F32),
            pltpu.VMEM((heads, tokens), F32),
            pltpu.VMEM(x_kernel.shape, F32),
            pltpu.VMEM(bc_kernel.shape, F32),
            pltpu.VMEM((1, channels), F32),
            pltpu.VMEM(bc_bias.shape, F32),
            pltpu.VMEM((1, heads), F32),
            pltpu.VMEM((tokens + HALO, channels), BF16),
            pltpu.VMEM((tokens, channels), BF16),
            pltpu.VMEM((chunks, CHUNK + STATE, channels), BF16),
            pltpu.VMEM((tokens, channels), BF16),
            pltpu.VMEM((2 * heads, channels), BF16),
            pltpu.VMEM((24, channels), F32),
            pltpu.VMEM((chunks, CHUNK, 2 * heads), BF16),
            pltpu.VMEM((chunks, CHUNK, 2 * heads), BF16),
            pltpu.VMEM((chunks, CHUNK, 2 * heads), BF16),
            pltpu.VMEM((3 * CHUNK, CHUNK + HALO), BF16),
            pltpu.VMEM((tokens, 2, STATE), BF16),
            pltpu.VMEM((2 * share, STATE), F32),
            pltpu.VMEM((2, n_head, share, STATE), BF16),
            pltpu.VMEM((2, tokens + HALO, STATE), BF16),
            pltpu.VMEM((tokens, STATE), BF16),
            pltpu.VMEM((chunks, STATE, CHUNK), BF16),
            pltpu.VMEM((chunks, CHUNK, CHUNK + STATE), BF16),
            pltpu.VMEM((PARTS, n_ctx, height, 128), BF16),
            pltpu.VMEM((PARTS, n_ctx, height, 128), BF16),
            pltpu.VMEM((PARTS, n_ctx, height, 128), BF16),
            pltpu.VMEM((1, 128), F32),
            pltpu.VMEM((n_ctx, 1, 128), F32),
            pltpu.VMEM((PARTS, n_ctx, 128), F32),
            dma((7,)), dma((chunks,)), dma, dma((n_head,)), dma((4,)), dma((2,)), dma((4,)), dma((2,)),
            dma((2 * PARTS,)), dma((2 * PARTS,)),
        ],
        compiler_params=pltpu.CompilerParams(
            collective_id=0, has_side_effects=True, vmem_limit_bytes=45_370_000
        ),
        cost_estimate=pl.CostEstimate(flops=2_500_000_000, bytes_accessed=10_000_000, transcendentals=5_000_000),
    )(x_in, bc_in, z_in, dt.T, log_decay.T, x_kernel, bc_kernel, x_bias[None], bc_bias, skip[None])
    return pl.pallas_call(
        finish,
        out_shape=jax.ShapeDtypeStruct((tokens, channels), BF16),
        in_specs=[vmem] * 6,
        out_specs=anywhere,
        scratch_shapes=[
            pltpu.VMEM((tokens, channels - channels // PARTS), F32),
            pltpu.VMEM((tokens, channels), BF16),
            dma((chunks,)),
        ],
        compiler_params=pltpu.CompilerParams(vmem_limit_bytes=16 * 1024 * 1024),
        cost_estimate=pl.CostEstimate(flops=600_000_000, bytes_accessed=4_000_000, transcendentals=1_000),
    )(a, b, c_part, ent, square, norm_gain[None])


def solution(mesh):
    placed = (
        P("ctx", "head"),
        P(("ctx", "head"), None, None),
        P("ctx", "head"),
        P("ctx", "head"),
        P("ctx", "head"),
        P(None, "head"),
        P(None, None, "head"),
        P("head"),
        P(None, "head"),
        P("head"),
        P("head"),
    )
    return jax.shard_map(
        functools.partial(per_device, mesh.shape["ctx"], mesh.shape["head"]),
        mesh=mesh, in_specs=placed, out_specs=P("ctx", "head"), check_vma=False,
    )
```

```python
import functools

import jax
import jax.numpy as jnp
from jax import lax
from jax.experimental import pallas as pl
from jax.experimental.pallas import tpu as pltpu
from jax.sharding import PartitionSpec as P

MESH = pl.DeviceIdType.MESH
F32, BF16 = jnp.float32, jnp.bfloat16
HEAD_DIM = 64
STATE = 128
CHUNK = 128
HALO = 16
WIDE = 256
PARTS = 2
HIGHEST = lax.Precision.HIGHEST


def split(value):
    high = value.astype(BF16)
    low = (value - high.astype(F32)).astype(BF16)
    return jnp.concatenate([high, low], axis=0)


def split_columns(value):
    high = value.astype(BF16).astype(F32)
    return jnp.concatenate([high, value - high], axis=0).T.astype(BF16)


def across(left, right):
    return lax.dot_general(left, right, (((0,), (0,)), ((), ())), preferred_element_type=F32)


def dot(left, right):
    return jnp.dot(left, right, preferred_element_type=F32)


def swish_of_twice(half):
    return half + half * jnp.tanh(half)


def kernel(
    sizes,
    x_hbm, bc_hbm, z_hbm, dt_hbm, decay_hbm, xk_hbm, bck_hbm, xb_hbm, bcb_hbm, skip_hbm,
    a_buf, b_buf, c_buf, ent, square_buf,
    dt_ref, decay_ref, xk_ref, bck_ref, xb_ref, bcb_ref, skip_ref,
    x_buf, xc_buf, xs_buf, z_buf,
    spread, rows, w_t, g_t, full_t, shift, bc_raw, bc_f32, bc_send, bc_buf, b_conv, b_t, sc_buf,
    f_buf, r_buf, o_buf, d_send, d_buf, e_decay,
    small_sem, x_sem, z_sem, raw_sem, bc_sem, hx_sem, hb_sem, d_sem, f_sem, e_sem,
):
    n_ctx, n_head, tokens, channels = sizes
    chunks, tiles = tokens // CHUNK, channels // WIDE
    heads = channels // HEAD_DIM
    share = tokens // n_head
    c, h = lax.axis_index("ctx"), lax.axis_index("head")
    following, preceding = lax.rem(c + 1, n_ctx), lax.rem(c + n_ctx - 1, n_ctx)
    last_head = n_head - 1

    barrier = pltpu.get_barrier_semaphore()

    @pl.loop(1, n_head)
    def _(d):
        pl.semaphore_signal(barrier, inc=1, device_id=(c, lax.rem(h + d, n_head)), device_id_type=MESH)

    @pl.when(h != last_head)
    def _():
        pl.semaphore_signal(barrier, inc=1, device_id=(preceding, last_head), device_id_type=MESH)

    @pl.loop(1, n_ctx)
    def _(d):
        pl.semaphore_signal(barrier, inc=1, device_id=(lax.rem(c + d, n_ctx), h), device_id_type=MESH)

    def columns(t):
        return pl.ds(pl.multiple_of(t * STATE, STATE), STATE)

    def raw_copy(t):
        return pltpu.make_async_copy(
            bc_hbm.at[:, :, t * STATE : (t + 1) * STATE], bc_raw.at[pl.ds(t * share, share)], raw_sem.at[t]
        )

    def x_copy(q):
        part = pl.ds(q * CHUNK, CHUNK)
        return pltpu.make_async_copy(
            x_hbm.at[part], x_buf.at[pl.ds(HALO + q * CHUNK, CHUNK)], x_sem.at[q]
        )

    small = [
        pltpu.make_async_copy(source, target, small_sem.at[i])
        for i, (source, target) in enumerate((
            (decay_hbm, decay_ref), (dt_hbm, dt_ref), (skip_hbm, skip_ref), (xk_hbm, xk_ref), (xb_hbm, xb_ref),
            (bck_hbm, bck_ref), (bcb_hbm, bcb_ref),
        ))
    ]
    small[0].start()
    for t in range(n_head):
        raw_copy(t).start()
    for copy in small[1:]:
        copy.start()
    for q in range(chunks):
        x_copy(q).start()
    z_copy = pltpu.make_async_copy(z_hbm, z_buf, z_sem)
    z_copy.start()

    d_send[...] = jnp.zeros_like(d_send)
    small[0].wait()
    sums = lax.dot_general(
        jnp.ones((8, tokens), F32), decay_ref[...], (((1,), (1,)), ((), ())),
        precision=HIGHEST, preferred_element_type=F32,
    )
    d_send[:, 0:heads] = sums[0:1]
    d_buf[c] = d_send[...]

    flat = bc_raw.reshape(2 * tokens, STATE)
    for t in range(n_head):
        raw_copy(t).wait()
        bc_f32[...] = flat[2 * t * share : 2 * (t + 1) * share].astype(F32)
        for which in range(2):
            bc_send[which, t] = bc_f32[pl.ds(which, share, stride=2), :].astype(BF16)

    head_of = lax.broadcasted_iota(jnp.int32, (2 * heads, channels), 1) // HEAD_DIM
    row_of = lax.rem(lax.broadcasted_iota(jnp.int32, (2 * heads, channels), 0), heads)
    spread[...] = (head_of == row_of).astype(F32).astype(BF16)

    for copy in small[1:]:
        copy.wait()

    upto = (
        lax.broadcasted_iota(jnp.int32, (CHUNK, CHUNK), 0) <= lax.broadcasted_iota(jnp.int32, (CHUNK, CHUNK), 1)
    ).astype(F32)
    before = jnp.zeros((heads, 1), F32)
    to_middle, to_end = [], []
    for q in range(chunks):
        part = slice(q * CHUNK, (q + 1) * CHUNK)
        cum = jnp.dot(decay_ref[:, part], upto, precision=HIGHEST, preferred_element_type=F32)
        middle, last = cum[:, CHUNK // 2 - 1 : CHUNK // 2], cum[:, CHUNK - 1 : CHUNK]
        w_t[q] = split_columns(jnp.exp(middle - cum) * dt_ref[:, part])
        g_t[q] = split_columns(jnp.exp(cum - middle))
        full_t[q] = split_columns(jnp.exp(before + cum))
        to_middle.append(jnp.exp(middle))
        to_end.append(jnp.exp(last - middle))
        before = before + last
    lane = lax.broadcasted_iota(jnp.int32, (heads, 128), 1)
    packed = jnp.zeros((heads, 128), F32)
    for i, value in enumerate(to_middle + to_end):
        packed = jnp.where(lane == i, value, packed)
    eye = lax.broadcasted_iota(jnp.int32, (heads, heads), 0) == lax.broadcasted_iota(jnp.int32, (heads, heads), 1)
    skip_column = jnp.sum(jnp.where(eye, skip_ref[...], 0.0), axis=1, keepdims=True)
    packed = split(jnp.where(lane == 2 * chunks, skip_column, packed))
    for j in range(tiles):
        wide = slice(j * WIDE, (j + 1) * WIDE)
        rows[:, wide] = across(packed, spread[:, wide])[0 : rows.shape[0]]

    row = lax.broadcasted_iota(jnp.int32, shift.shape, 0)
    column = lax.broadcasted_iota(jnp.int32, shift.shape, 1)
    shift[...] = (column == lax.rem(row, CHUNK) + row // CHUNK + HALO - 3).astype(F32).astype(BF16)

    pl.semaphore_wait(barrier, n_ctx - 1 + n_head - 1 + jnp.where(h == last_head, n_head - 1, 0))

    mine = pl.ds(pl.multiple_of(HALO + h * share, HALO), share)
    halo_x = pltpu.make_async_remote_copy(
        src_ref=x_hbm.at[pl.ds(tokens - HALO, HALO)], dst_ref=x_buf.at[pl.ds(0, HALO)],
        send_sem=hx_sem.at[0], recv_sem=hx_sem.at[1], device_id=(following, h), device_id_type=MESH,
    )

    def share_out(which):
        for d in sorted(range(1, n_head), key=lambda d: (-min(d, n_head - d), d)):
            t = lax.rem(h + d, n_head)
            pltpu.make_async_remote_copy(
                src_ref=bc_send.at[which, t], dst_ref=bc_buf.at[which, mine],
                send_sem=bc_sem.at[2 * which], recv_sem=bc_sem.at[2 * which + 1],
                device_id=(c, t), device_id_type=MESH,
            ).start()

        @pl.when(h == last_head)
        def _():
            @pl.loop(0, n_head)
            def _(t):
                pltpu.make_async_remote_copy(
                    src_ref=bc_send.at[which, t, pl.ds(share - HALO, HALO)], dst_ref=bc_buf.at[which, pl.ds(0, HALO)],
                    send_sem=hb_sem.at[2 * which], recv_sem=hb_sem.at[2 * which + 1],
                    device_id=(following, t), device_id_type=MESH,
                ).start()

        bc_buf[which, mine] = bc_send[which, h]

    share_out(0)
    halo_x.start()

    @pl.loop(1, n_ctx)
    def _(d):
        pltpu.make_async_remote_copy(
            src_ref=d_send, dst_ref=d_buf.at[c], send_sem=d_sem.at[0], recv_sem=d_sem.at[1],
            device_id=(lax.rem(c + d, n_ctx), h), device_id_type=MESH,
        ).start()

    x_copy(0).wait()

    @pl.loop(0, chunks)
    def _(i):
        q = lax.rem(i + 1, chunks)

        @pl.when(q != 0)
        def _():
            x_copy(q).wait()

        @pl.when(q == 0)
        def _():
            halo_x.wait_recv()

            @pl.when(c == 0)
            def _():
                x_buf[0:HALO] = jnp.zeros((HALO, channels), BF16)

        part = pl.ds(pl.multiple_of(q * CHUNK, CHUNK), CHUNK)
        around = pl.ds(pl.multiple_of(q * CHUNK, CHUNK), CHUNK + HALO)
        for j in range(tiles):
            wide = slice(j * WIDE, (j + 1) * WIDE)
            seen = x_buf[around, wide]
            moved = dot(shift[...], seen)
            half = 0.5 * xb_ref[:, wide] + (0.5 * xk_ref[3:4, wide]) * seen[HALO:].astype(F32)
            for tap in range(3):
                half = half + (0.5 * xk_ref[tap : tap + 1, wide]) * moved[tap * CHUNK : (tap + 1) * CHUNK]
            xc = swish_of_twice(half)
            xc_buf[part, wide] = xc.astype(BF16)
            xs_buf[q, 0:CHUNK, wide] = (xc * dot(w_t[q], spread[:, wide])).astype(BF16)

    def others(which):
        return bc_buf.at[which, pl.ds(0, tokens - share)]

    def arrived(which):
        pltpu.make_async_copy(others(which), others(which), bc_sem.at[2 * which + 1]).wait()
        rim = bc_buf.at[which, pl.ds(0, HALO)]
        pltpu.make_async_copy(rim, rim, hb_sem.at[2 * which + 1]).wait()

        @pl.when(c == 0)
        def _():
            bc_buf[which, 0:HALO] = jnp.zeros((HALO, STATE), BF16)

    def convolved(which, q):
        seen = bc_buf[which, q * CHUNK : q * CHUNK + CHUNK + HALO]
        moved = dot(shift[...], seen)
        half = 0.5 * bcb_ref[which : which + 1] + (0.5 * bck_ref[3, which : which + 1]) * seen[HALO:].astype(F32)
        for tap in range(3):
            half = half + (0.5 * bck_ref[tap, which : which + 1]) * moved[tap * CHUNK : (tap + 1) * CHUNK]
        return swish_of_twice(half)

    arrived(0)
    share_out(1)
    for q in range(chunks):
        b_part = convolved(0, q)
        b_conv[q * CHUNK : (q + 1) * CHUNK] = b_part.astype(BF16)
        b_t[q] = b_part.T.astype(BF16)

    deep = n_ctx * 128 * PARTS // channels
    height = STATE // deep
    part_tiles = tiles // PARTS
    per_tile = n_ctx // part_tiles

    def to_owner(p, k):
        return pltpu.make_async_remote_copy(
            src_ref=f_buf.at[p, k], dst_ref=r_buf.at[p, c], send_sem=f_sem.at[2 * p], recv_sem=f_sem.at[2 * p + 1],
            device_id=(k, h), device_id_type=MESH,
        )

    for p in range(PARTS):
        @pl.loop(0, part_tiles)
        def _(i):
            j = lax.rem(i + c // per_tile, part_tiles)
            wide = pl.ds(pl.multiple_of((p * part_tiles + j) * WIDE, WIDE), WIDE)
            state = jnp.zeros((STATE, WIDE), F32)
            for q in range(chunks):
                scaled = state * rows[q : q + 1, wide]
                xs_buf[q, CHUNK : CHUNK + STATE, wide] = scaled.astype(BF16)
                fresh = dot(b_t[q], xs_buf[q, 0:CHUNK, wide])
                state = (scaled + fresh) * rows[chunks + q : chunks + q + 1, wide]
            for a in range(WIDE // 128):
                for b in range(deep):
                    f_buf[p, j * per_tile + a * deep + b] = state[
                        b * height : (b + 1) * height, a * 128 : (a + 1) * 128
                    ].astype(BF16)

            @pl.loop(0, per_tile)
            def _(s):
                k = j * per_tile + s

                @pl.when(k != c)
                def _():
                    to_owner(p, k).start()

        r_buf[p, c] = f_buf[p, c]

    arrived(1)
    causal = lax.broadcasted_iota(jnp.int32, (CHUNK, CHUNK), 0) >= lax.broadcasted_iota(jnp.int32, (CHUNK, CHUNK), 1)
    for q in range(chunks):
        b_part, c_part = b_conv[q * CHUNK : (q + 1) * CHUNK], convolved(1, q).astype(BF16)
        scores = lax.dot_general(c_part, b_part, (((1,), (1,)), ((), ())), preferred_element_type=F32)
        sc_buf[q, :, 0:CHUNK] = jnp.where(causal, scores, 0.0).astype(BF16)
        sc_buf[q, :, CHUNK : CHUNK + STATE] = c_part
        c_buf[q * CHUNK : (q + 1) * CHUNK] = c_part
    z_copy.wait()

    def gate(first, end):
        @pl.loop(first, end)
        def _(q):
            part = pl.ds(pl.multiple_of(q * CHUNK, CHUNK), CHUNK)
            for j in range(tiles):
                wide = slice(j * WIDE, (j + 1) * WIDE)
                y = dot(sc_buf[q], xs_buf[q, :, wide]) * dot(g_t[q], spread[:, wide])
                y = y + rows[2 * chunks : 2 * chunks + 1, wide] * xc_buf[part, wide].astype(F32)
                swish = swish_of_twice(0.5 * z_buf[part, wide].astype(F32))
                a_buf[part, wide] = y * swish
                b_buf[part, wide] = dot(full_t[q], spread[:, wide]) * swish

    pltpu.make_async_copy(d_buf.at[pl.ds(0, n_ctx - 1)], d_buf.at[pl.ds(0, n_ctx - 1)], d_sem.at[1]).wait()
    totals = d_buf[...].reshape(n_ctx, 128)

    def pair(p):
        return p * (channels // 128 // PARTS) + c // deep

    for p in range(PARTS):
        pick = (
            lax.broadcasted_iota(jnp.int32, (128, 128), 0)
            == 2 * pair(p) + lax.broadcasted_iota(jnp.int32, (128, 128), 1) // HEAD_DIM
        ).astype(F32)
        e_decay[p] = jnp.exp(jnp.dot(totals, pick, precision=HIGHEST, preferred_element_type=F32))

    def scan(p):
        pltpu.make_async_copy(
            r_buf.at[p, pl.ds(0, n_ctx - 1)], r_buf.at[p, pl.ds(0, n_ctx - 1)], f_sem.at[2 * p + 1]
        ).wait()

        state = jnp.zeros((height, 128), F32)
        for i in range(n_ctx):
            o_buf[p, i] = state.astype(BF16)
            state = state * e_decay[p, i : i + 1, :] + r_buf[p, i].astype(F32)

        place = (
            pl.ds(pl.multiple_of(lax.rem(c, deep) * height, height), height),
            pl.ds(pl.multiple_of(pair(p) * 128, 128), 128),
        )

        for d in sorted(range(1, n_ctx), key=lambda d: (-min(d % 8, 8 - d % 8), d)):
            t = lax.rem(c + d, n_ctx)
            pltpu.make_async_remote_copy(
                src_ref=o_buf.at[p, t], dst_ref=ent.at[place], send_sem=e_sem.at[2 * p], recv_sem=e_sem.at[2 * p + 1],
                device_id=(t, h), device_id_type=MESH,
            ).start()

        ent[place] = o_buf[p, c]

    def entered(p):
        pltpu.make_async_copy(
            o_buf.at[p, pl.ds(0, n_ctx - 1)], o_buf.at[p, pl.ds(0, n_ctx - 1)], e_sem.at[2 * p + 1]
        ).wait()

    gate(0, chunks // 2)
    scan(0)
    gate(chunks // 2, chunks - 1)
    scan(1)
    gate(chunks - 1, chunks)

    entered(0)

    @pl.loop(0, chunks)
    def _(q):
        part = pl.ds(pl.multiple_of(q * CHUNK, CHUNK), CHUNK)
        square = jnp.zeros((CHUNK, WIDE), F32)
        for j in range(part_tiles):
            wide = slice(j * WIDE, (j + 1) * WIDE)
            gated = a_buf[part, wide] + b_buf[part, wide] * dot(c_buf[part], ent[:, wide])
            a_buf[part, wide] = gated
            square = square + gated * gated
        square_buf[part] = square[:, : WIDE // 2] + square[:, WIDE // 2 :]

    for p in range(1, PARTS):
        entered(p)

    for which in range(2):
        pltpu.make_async_copy(others(which), others(which), bc_sem.at[2 * which]).wait()

    @pl.when(h == last_head)
    def _():
        for which in range(2):
            sent = bc_buf.at[which, pl.ds(0, n_head * HALO)]
            pltpu.make_async_copy(sent, sent, hb_sem.at[2 * which]).wait()

    halo_x.wait_send()
    sent = d_buf.at[pl.ds(0, n_ctx - 1)]
    pltpu.make_async_copy(sent, sent, d_sem.at[0]).wait()
    for buffer, sem in ((f_buf, f_sem), (o_buf, e_sem)):
        for p in range(PARTS):
            sent = buffer.at[p, pl.ds(0, n_ctx - 1)]
            pltpu.make_async_copy(sent, sent, sem.at[2 * p]).wait()


def finish(a_ref, b_ref, c_ref, ent_ref, square_ref, gain_ref, out_hbm, g_buf, out_buf, out_sem):
    tokens, channels = a_ref.shape
    chunks, tiles = tokens // CHUNK, channels // WIDE

    def out_copy(q):
        part = pl.ds(q * CHUNK, CHUNK)
        return pltpu.make_async_copy(out_buf.at[part], out_hbm.at[part], out_sem.at[q])

    first = tiles // PARTS * WIDE
    for q in range(chunks):
        part = slice(q * CHUNK, (q + 1) * CHUNK)
        square = square_ref[part]
        for j in range(tiles // PARTS, tiles):
            wide = slice(j * WIDE, (j + 1) * WIDE)
            gated = a_ref[part, wide] + b_ref[part, wide] * dot(c_ref[part], ent_ref[:, wide])
            g_buf[part, wide.start - first : wide.stop - first] = gated
            squared = gated * gated
            square = square + squared[:, : WIDE // 2] + squared[:, WIDE // 2 :]
        scale = lax.rsqrt(jnp.sum(square, axis=1, keepdims=True) * (1.0 / channels) + 1e-5)
        for j in range(tiles):
            wide = slice(j * WIDE, (j + 1) * WIDE)
            if j < tiles // PARTS:
                gated = a_ref[part, wide]
            else:
                gated = g_buf[part, wide.start - first : wide.stop - first]
            out_buf[part, wide] = (gated * scale * gain_ref[:, wide]).astype(BF16)
        out_copy(q).start()

    for q in range(chunks):
        out_copy(q).wait()


def per_device(
    n_ctx, n_head, x_in, bc_in, z_in, dt, log_decay, x_kernel, bc_kernel, x_bias, bc_bias, skip, norm_gain
):
    tokens, channels = x_in.shape
    heads = channels // HEAD_DIM
    chunks = tokens // CHUNK
    height = STATE * channels // PARTS // n_ctx // 128
    share = tokens // n_head
    anywhere, vmem = pl.BlockSpec(memory_space=pl.ANY), pl.BlockSpec(memory_space=pltpu.VMEM)
    dma = pltpu.SemaphoreType.DMA
    a, b, c_part, ent, square = pl.pallas_call(
        functools.partial(kernel, (n_ctx, n_head, tokens, channels)),
        out_shape=[
            pltpu.VMEM((tokens, channels), F32),
            pltpu.VMEM((tokens, channels), F32),
            pltpu.VMEM((tokens, STATE), BF16),
            pltpu.VMEM((STATE, channels), BF16),
            pltpu.VMEM((tokens, WIDE // 2), F32),
        ],
        in_specs=[anywhere] * 10,
        out_specs=[vmem] * 5,
        scratch_shapes=[
            pltpu.VMEM((heads, tokens), F32),
            pltpu.VMEM((heads, tokens), F32),
            pltpu.VMEM(x_kernel.shape, F32),
            pltpu.VMEM(bc_kernel.shape, F32),
            pltpu.VMEM((1, channels), F32),
            pltpu.VMEM(bc_bias.shape, F32),
            pltpu.VMEM((1, heads), F32),
            pltpu.VMEM((tokens + HALO, channels), BF16),
            pltpu.VMEM((tokens, channels), BF16),
            pltpu.VMEM((chunks, CHUNK + STATE, channels), BF16),
            pltpu.VMEM((tokens, channels), BF16),
            pltpu.VMEM((2 * heads, channels), BF16),
            pltpu.VMEM((24, channels), F32),
            pltpu.VMEM((chunks, CHUNK, 2 * heads), BF16),
            pltpu.VMEM((chunks, CHUNK, 2 * heads), BF16),
            pltpu.VMEM((chunks, CHUNK, 2 * heads), BF16),
            pltpu.VMEM((3 * CHUNK, CHUNK + HALO), BF16),
            pltpu.VMEM((tokens, 2, STATE), BF16),
            pltpu.VMEM((2 * share, STATE), F32),
            pltpu.VMEM((2, n_head, share, STATE), BF16),
            pltpu.VMEM((2, tokens + HALO, STATE), BF16),
            pltpu.VMEM((tokens, STATE), BF16),
            pltpu.VMEM((chunks, STATE, CHUNK), BF16),
            pltpu.VMEM((chunks, CHUNK, CHUNK + STATE), BF16),
            pltpu.VMEM((PARTS, n_ctx, height, 128), BF16),
            pltpu.VMEM((PARTS, n_ctx, height, 128), BF16),
            pltpu.VMEM((PARTS, n_ctx, height, 128), BF16),
            pltpu.VMEM((1, 128), F32),
            pltpu.VMEM((n_ctx, 1, 128), F32),
            pltpu.VMEM((PARTS, n_ctx, 128), F32),
            dma((7,)), dma((chunks,)), dma, dma((n_head,)), dma((4,)), dma((2,)), dma((4,)), dma((2,)),
            dma((2 * PARTS,)), dma((2 * PARTS,)),
        ],
        compiler_params=pltpu.CompilerParams(
            collective_id=0, has_side_effects=True, vmem_limit_bytes=45_370_000
        ),
        cost_estimate=pl.CostEstimate(flops=2_500_000_000, bytes_accessed=10_000_000, transcendentals=5_000_000),
    )(x_in, bc_in, z_in, dt.T, log_decay.T, x_kernel, bc_kernel, x_bias[None], bc_bias, skip[None])
    return pl.pallas_call(
        finish,
        out_shape=jax.ShapeDtypeStruct((tokens, channels), BF16),
        in_specs=[vmem] * 6,
        out_specs=anywhere,
        scratch_shapes=[
            pltpu.VMEM((tokens, channels - channels // PARTS), F32),
            pltpu.VMEM((tokens, channels), BF16),
            dma((chunks,)),
        ],
        compiler_params=pltpu.CompilerParams(vmem_limit_bytes=16 * 1024 * 1024),
        cost_estimate=pl.CostEstimate(flops=600_000_000, bytes_accessed=4_000_000, transcendentals=1_000),
    )(a, b, c_part, ent, square, norm_gain[None])


def solution(mesh):
    placed = (
        P("ctx", "head"),
        P(("ctx", "head"), None, None),
        P("ctx", "head"),
        P("ctx", "head"),
        P("ctx", "head"),
        P(None, "head"),
        P(None, None, "head"),
        P("head"),
        P(None, "head"),
        P("head"),
        P("head"),
    )
    return jax.shard_map(
        functools.partial(per_device, mesh.shape["ctx"], mesh.shape["head"]),
        mesh=mesh, in_specs=placed, out_specs=P("ctx", "head"), check_vma=False,
    )
```
